256 devices in a mesh: tile: 64 (over y, z, core), grp: 4 (over x).
Axes of the slice: x: 4, y: 4, z: 8, core: 2. Of those that a mesh axis runs over, the one named last changes fastest.
Arguments:
- noisy: bfloat16 [4, 7, 4096, 256], P(None, None, ('tile', 'grp')), may hold values from -6 to 6
- state_0: bfloat16 [32, 4096, 256], P(None, ('tile', 'grp')), may hold values from -6 to 6
- state_1: bfloat16 [43, 2048, 128], P(None, ('tile', 'grp')), may hold values from -6 to 6
- state_2: bfloat16 [57, 1024, 64], P(None, ('tile', 'grp')), may hold values from -6 to 6
- state_3: bfloat16 [76, 512, 32], P(None, ('tile', 'grp')), may hold values from -6 to 6
- state_4: bfloat16 [101, 256, 16], P(None, ('tile', 'grp')), may hold values from -6 to 6
- enc_in_0: bfloat16 [9, 32, 7], replicated, may hold values from -0.75 to 0.75
- enc_in_1: bfloat16 [9, 43, 32], replicated, may hold values from -0.375 to 0.375
- enc_in_2: bfloat16 [9, 57, 43], replicated, may hold values from -0.3125 to 0.3125
- enc_in_3: bfloat16 [9, 76, 57], replicated, may hold values from -0.25 to 0.25
- enc_in_4: bfloat16 [9, 101, 76], replicated, may hold values from -0.21875 to 0.21875
- enc_rec_0: bfloat16 [9, 32, 64], replicated, may hold values from -0.375 to 0.375
- enc_rec_1: bfloat16 [9, 43, 86], replicated, may hold values from -0.3125 to 0.3125
- enc_rec_2: bfloat16 [9, 57, 114], replicated, may hold values from -0.25 to 0.25
- enc_rec_3: bfloat16 [9, 76, 152], replicated, may hold values from -0.21875 to 0.21875
- enc_rec_4: bfloat16 [9, 101, 202], replicated, may hold values from -0.1875 to 0.1875
- dec_0: bfloat16 [9, 32, 75], replicated, may hold values from -0.25 to 0.25
- dec_1: bfloat16 [9, 43, 100], replicated, may hold values from -0.1875 to 0.1875
- dec_2: bfloat16 [9, 57, 133], replicated, may hold values from -0.1875 to 0.1875
- dec_3: bfloat16 [9, 76, 177], replicated, may hold values from -0.15625 to 0.15625
- out_weight: bfloat16 [9, 3, 32], replicated, may hold values from -0.375 to 0.375
Outputs:
- denoised: float32 [4, 3, 4096, 256], P(None, None, ('tile', 'grp'))
- final_state: bfloat16 [101, 256, 16], P(None, ('tile', 'grp'))
The draws below stay inside these ranges and needn't reach their ends.
All inputs are finite; a program needn't handle non-finite values.
Results may differ from the reference program's by a relative error of at most 0.025.
Values may be sent and summed in bfloat16 or wider, within the bound.
No kernel may reach another device: no remote copies, remote signals or barrier semaphores. Data moves between devices by JAX's collectives and lax.ppermute only.
A program may use at most 64 MiB of HBM per device.

```python
import jax
import jax.numpy as jnp

CIN = 7
C0 = 32
C1 = 43
C2 = 57
C3 = 76
C4 = 101
WIDTH = 256
FRAMES = 4
HEIGHT = 4096


def levels(rng, shape, shards, smallest, top_value):
    def one(dim, shards_of):
        heights = jax.random.uniform(jax.random.fold_in(jax.random.fold_in(rng, 6), dim), (shards_of,), jnp.float32, smallest / len(shards), top_value / len(shards))
        return jnp.repeat(jnp.exp(heights), shape[dim] // shards_of).reshape((-1,) + (1,) * (len(shape) - dim - 1))

    gain = one(*shards[0])
    for cut in shards[1:]:
        gain = gain * one(*cut)
    return gain


def noise(rng, dims, deviation, most, shards=(), kind=jnp.bfloat16):
    array = jax.random.normal(rng, dims, jnp.float32) * deviation
    if len(shards) > 0:
        array = levels(rng, dims, shards, -0.22, 0.18) * array
    return jnp.clip(array, min=-most, max=most).astype(kind)


def setup_inputs(seed: int = 0) -> dict:
    key_of = jax.random.split(jax.random.key(seed), 22)
    return {
        "noisy": noise(key_of[0], (FRAMES, CIN, HEIGHT, WIDTH), 1.0, 6.0, ((2, 256),)),
        "state_0": noise(key_of[1], (C0, HEIGHT, WIDTH), 1.0, 6.0, ((1, 256),)),
        "state_1": noise(key_of[2], (C1, HEIGHT // 2, WIDTH // 2), 1.0, 6.0, ((1, 256),)),
        "state_2": noise(key_of[3], (C2, HEIGHT // 4, WIDTH // 4), 1.0, 6.0, ((1, 256),)),
        "state_3": noise(key_of[4], (C3, HEIGHT // 8, WIDTH // 8), 1.0, 6.0, ((1, 256),)),
        "state_4": noise(key_of[5], (C4, HEIGHT // 16, WIDTH // 16), 1.0, 6.0, ((1, 256),)),
        "enc_in_0": noise(key_of[6], (9, C0, CIN), (9 * CIN) ** -0.5, 0.75),
        "enc_in_1": noise(key_of[7], (9, C1, C0), (9 * C0) ** -0.5, 0.375),
        "enc_in_2": noise(key_of[8], (9, C2, C1), (9 * C1) ** -0.5, 0.3125),
        "enc_in_3": noise(key_of[9], (9, C3, C2), (9 * C2) ** -0.5, 0.25),
        "enc_in_4": noise(key_of[10], (9, C4, C3), (9 * C3) ** -0.5, 0.21875),
        "enc_rec_0": noise(key_of[11], (9, C0, 2 * C0), (9 * C0) ** -0.5, 0.375),
        "enc_rec_1": noise(key_of[12], (9, C1, 2 * C1), (9 * C1) ** -0.5, 0.3125),
        "enc_rec_2": noise(key_of[13], (9, C2, 2 * C2), (9 * C2) ** -0.5, 0.25),
        "enc_rec_3": noise(key_of[14], (9, C3, 2 * C3), (9 * C3) ** -0.5, 0.21875),
        "enc_rec_4": noise(key_of[15], (9, C4, 2 * C4), (9 * C4) ** -0.5, 0.1875),
        "dec_0": noise(key_of[16], (9, C0, C1 + C0), (9 * (C1 + C0)) ** -0.5, 0.25),
        "dec_1": noise(key_of[17], (9, C1, C2 + C1), (9 * (C2 + C1)) ** -0.5, 0.1875),
        "dec_2": noise(key_of[18], (9, C2, C3 + C2), (9 * (C3 + C2)) ** -0.5, 0.1875),
        "dec_3": noise(key_of[19], (9, C3, C4 + C3), (9 * (C4 + C3)) ** -0.5, 0.15625),
        "out_weight": noise(key_of[20], (9, 3, C0), (9 * C0) ** -0.5, 0.375),
    }


def act(value):
    return jnp.where(value > 0, value, 0.1 * value).astype(jnp.bfloat16)


def conv(field, kernel):
    height, width = field.shape[1], field.shape[2]
    padded = jnp.pad(field, ((0, 0), (1, 1), (1, 1))).astype(jnp.float32)
    kernel32 = kernel.astype(jnp.float32)
    total = jnp.zeros((kernel.shape[1], height, width), jnp.float32)
    for offset in range(9):
        shift_r = offset // 3
        shift_c = offset % 3
        total = total + jnp.einsum("oc,chw->ohw", kernel32[offset], padded[:, shift_r:shift_r + height, shift_c:shift_c + width])
    return total


def shrink(field):
    chans, height, width = field.shape
    return field.reshape(chans, height // 2, 2, width // 2, 2).max(axis=(2, 4))


def enlarge(field):
    return jnp.repeat(jnp.repeat(field, 2, axis=1), 2, axis=2)


def reference(noisy, state_0, state_1, state_2, state_3, state_4, enc_in_0, enc_in_1, enc_in_2, enc_in_3, enc_in_4, enc_rec_0, enc_rec_1, enc_rec_2, enc_rec_3, enc_rec_4, dec_0, dec_1, dec_2, dec_3, out_weight):
    states = [state_0, state_1, state_2, state_3, state_4]
    inputs_w = [enc_in_0, enc_in_1, enc_in_2, enc_in_3, enc_in_4]
    recur_w = [enc_rec_0, enc_rec_1, enc_rec_2, enc_rec_3, enc_rec_4]
    decode_w = [dec_0, dec_1, dec_2, dec_3]
    results = []
    for frame in range(FRAMES):
        field = noisy[frame]
        skips = []
        for level in range(5):
            first = act(conv(field, inputs_w[level]))
            states[level] = act(conv(jnp.concatenate([first, states[level]], 0), recur_w[level]))
            skips.append(states[level])
            if level < 4:
                field = shrink(states[level])
        lower = skips[4]
        for level in range(3, -1, -1):
            lower = act(conv(jnp.concatenate([enlarge(lower), skips[level]], 0), decode_w[level]))
        results.append(conv(lower, out_weight))
    return jnp.stack(results), states[4]
```

```python
import functools

import jax
import jax.numpy as jnp
import numpy as np
from jax import lax
from jax.experimental import pallas as pl
from jax.experimental.pallas import tpu as pltpu
from jax.sharding import PartitionSpec as P

BF = jnp.bfloat16
F32 = jnp.float32
AXES = ("tile", "grp")
FRAMES = 4
C0, C1, C2, C3, C4 = 32, 48, 64, 80, 112
XROWS = FRAMES * C1
BLOCK = XROWS + C2 + 48
VMEM = 56 * 1024 * 1024
GROUP = 8


def taps(kernel, out_pad, parts):
    pieces, at = [], 0
    for chans, pad in parts:
        piece = kernel[:, :, at : at + chans]
        pieces.append(jnp.pad(piece, ((0, 0), (0, out_pad - kernel.shape[1]), (0, pad - chans))))
        at += chans
    full = jnp.concatenate(pieces, 2) if len(pieces) > 1 else pieces[0]
    depth = full.shape[2]
    full = full.reshape(3, 3, out_pad, depth).transpose(1, 2, 0, 3)
    return full.reshape(3 * out_pad, 3 * depth)


def two_rows(matrix, depth):
    zero = jnp.zeros((matrix.shape[0], depth), matrix.dtype)
    return jnp.concatenate(
        [jnp.concatenate([matrix, zero], 1), jnp.concatenate([zero, matrix], 1)], 0
    )


def pool_matrix(width, rows, lane_of):
    m = np.zeros((rows * width, 256), np.float32)
    for r in range(0, rows, 2):
        for c in range(0, width, 2):
            m[r * width + c, lane_of(r // 2, c // 2)] = 1
    return m


def selections():
    out = {}
    s0 = np.zeros((256, 128), np.float32)
    s0[2 * np.arange(128), np.arange(128)] = 1
    out["s0"] = s0
    s1 = np.zeros((4, 128, 256), np.float32)
    for j in range(4):
        s1[j, 2 * np.arange(64), 64 * j + np.arange(64)] = 1
    out["s1"] = s1.reshape(512, 256)
    out["s2"] = np.concatenate(
        [pool_matrix(64, 4, lambda r, c, i=i: 64 * i + 32 * r + c) for i in range(4)], 0
    )
    out["s3"] = np.concatenate(
        [pool_matrix(32, 8, lambda r, c, i=i: 64 * i + 16 * r + c) for i in range(4)], 0
    )
    u3 = np.zeros((256, 256), np.float32)
    for r in range(-4, 4):
        for c in range(32):
            u3[(r // 2 + 8) * 16 + c // 2, (r + 4) * 32 + c] = 1
    out["u3"] = u3
    u2 = np.zeros((256, 768), np.float32)
    for r in range(-4, 8):
        if -4 <= r // 2 < 4:
            for c in range(64):
                u2[(r // 2 + 4) * 32 + c // 2, (r + 4) * 64 + c] = 1
    out["u2"] = u2
    u1 = np.zeros((256, 512), np.float32)
    for r in range(4):
        for c in range(128):
            u1[r * 64 + c // 2, r * 128 + c] = 1
    out["u1"] = u1
    u0 = np.zeros((128, 256), np.float32)
    u0[np.arange(256) // 2, np.arange(256)] = 1
    out["u0"] = u0
    return {k: jnp.asarray(v, BF) for k, v in out.items()}


def dot(a, b):
    return jnp.dot(a, b, preferred_element_type=F32)


def lanes(shape):
    return lax.broadcasted_iota(jnp.int32, shape, 1)


def join_columns(y, out, width):
    count = y.shape[1]
    col = lanes((out, count)) & (width - 1)
    left = pltpu.roll(y[:out], 1, 1)
    right = pltpu.roll(y[2 * out :], count - 1, 1)
    return (
        y[out : 2 * out]
        + jnp.where(col == 0, 0.0, left)
        + jnp.where(col == width - 1, 0.0, right)
    )


def act(u):
    return jnp.maximum(u, 0.1 * u)


def three_rows(before, here, after, width):
    here32 = here.astype(F32)
    lane = lanes(here.shape)
    up = jnp.where(
        lane < width, pltpu.roll(before.astype(F32), width, 1), pltpu.roll(here32, width, 1)
    )
    down = jnp.where(
        lane >= 256 - width,
        pltpu.roll(after.astype(F32), 256 - width, 1),
        pltpu.roll(here32, 256 - width, 1),
    )
    return jnp.concatenate([up.astype(BF), here, down.astype(BF)], 0)


def three_rows_alone(here, width):
    here32 = here.astype(F32)
    up = pltpu.roll(here32, width, 1).astype(BF)
    down = pltpu.roll(here32, 256 - width, 1).astype(BF)
    return jnp.concatenate([up, here, down], 0)


def pair_max(value, width):
    count = value.shape[1]
    value = jnp.maximum(value, pltpu.roll(value, count - 1, 1))
    return jnp.maximum(value, pltpu.roll(value, count - width, 1))


def rounds(count, body, group):
    def run(first, size):
        for store in [body(first + j) for j in range(size)]:
            store()

    full = count // group

    def step(i, carry):
        run(i * group, group)
        return carry

    lax.fori_loop(0, full, step, 0)
    if count % group:
        run(full * group, count % group)


def fine_kernel(
    pos, own, up, down, rest, t_in0, t_rec0, t_in1, t_rec1, s0, s1,
    block, skip0, skip1, n, xs0, m0, x1, xs1,
):
    dev = pos[0]
    has_up = (dev > 0).astype(F32)
    has_down = (dev < 255).astype(F32)

    def place(src, part):
        for f in range(FRAMES):
            n[f, part * 8 : part * 8 + 8] = src[f * 128 : f * 128 + 128].reshape(8, 16, 256)
        xs0[0, part * 16 : part * 16 + 16, C0:] = src[512:1024].reshape(16, C0, 256)
        for j in range(4):
            two = src[1024 + j * C1 : 1024 + (j + 1) * C1]
            xs1[0, part * 8 + 2 * j, C1:] = two[:, :128]
            xs1[0, part * 8 + 2 * j + 1, C1:] = two[:, 128:]

    place(up, 0)
    place(own, 1)
    place(down, 2)

    block[XROWS:] = rest[...]

    for f in range(FRAMES):
        now, new = f % 2, (f + 1) % 2
        halo = 14 - 2 * f

        def in0(i, f=f, now=now, halo=halo):
            r = 16 - (halo + 1) + 2 * i
            p = (r - 1) // 2
            rhs = n[f, pl.ds(p, 2)].reshape(32, 256)
            y = dot(t_in0[...], rhs)
            both = []
            for m in range(2):
                v = act(join_columns(y[m * 96 : m * 96 + 96], C0, 256))
                row = r + m
                keep = jnp.where(row < 16, has_up, jnp.where(row >= 32, has_down, 1.0))
                both.append((v * keep).astype(BF))

            def store():
                for m in range(2):
                    xs0[now, r + m, :C0] = both[m]

            return store

        rounds(8 + halo + 1, in0, GROUP)

        def rec0(i, f=f, now=now, new=new, halo=halo):
            r = 16 - halo + 2 * i
            rhs = xs0[now, pl.ds(r - 1, 4)].reshape(256, 256)
            y = dot(t_rec0[...], rhs)
            keep = jnp.where(r < 16, has_up, jnp.where(r >= 32, has_down, 1.0))
            both = []
            for m in range(2):
                v = act(join_columns(y[m * 96 : m * 96 + 96], C0, 256)) * keep
                both.append(v)
            top = jnp.maximum(both[0], both[1])
            top = jnp.maximum(top, pltpu.roll(top, 255, 1)).astype(BF)

            def store():
                for m in range(2):
                    xs0[new, r + m, C0:] = both[m].astype(BF)
                m0[i] = top

            return store

        rounds(8 + halo, rec0, GROUP)

        skip0[f] = xs0[new, 14:34, C0:]
        count = 8 + halo
        x1[:count] = dot(m0[:count].reshape(count * C0, 256), s0[...]).astype(BF).reshape(
            count, C0, 128
        )

        half = 5 - f

        def in1(i, f=f, now=now, half=half):
            left = x1[pl.ds(2 * i, 3)].reshape(3 * C0, 128)
            right = x1[pl.ds(2 * i + 1, 3)].reshape(3 * C0, 128)
            y = dot(t_in1[...], jnp.concatenate([left, right], 1))
            v = act(join_columns(y, C1, 128))
            both = []
            for m in range(2):
                row = 8 - (half + 1) + 2 * i + m
                keep = jnp.where(row < 8, has_up, jnp.where(row >= 16, has_down, 1.0))
                both.append((v[:, m * 128 : m * 128 + 128] * keep).astype(BF))

            def store():
                for m in range(2):
                    xs1[now, 8 - (half + 1) + 2 * i + m, :C1] = both[m]

            return store

        rounds(4 + half + 1, in1, GROUP)

        def rec1(i, f=f, now=now, new=new, half=half):
            r = 8 - half + 2 * i
            left = xs1[now, pl.ds(r - 1, 3)].reshape(6 * C1, 128)
            right = xs1[now, pl.ds(r, 3)].reshape(6 * C1, 128)
            y = dot(t_rec1[...], jnp.concatenate([left, right], 1))
            v = act(join_columns(y, C1, 128))
            both = []
            for m in range(2):
                row = r + m
                keep = jnp.where(row < 8, has_up, jnp.where(row >= 16, has_down, 1.0))
                both.append((v[:, m * 128 : m * 128 + 128] * keep).astype(BF))

            def store():
                for m in range(2):
                    xs1[new, r + m, C1:] = both[m]

            return store

        rounds(4 + half, rec1, GROUP)

        skip1[f] = xs1[new, 6:18, C1:]
        pooled = []
        for j in range(4):
            a = xs1[new, 8 + 2 * j, C1:].astype(F32)
            b = xs1[new, 9 + 2 * j, C1:].astype(F32)
            top = jnp.maximum(a, b)
            pooled.append(jnp.maximum(top, pltpu.roll(top, 127, 1)).astype(BF))
        block[f * C1 : f * C1 + C1] = dot(jnp.concatenate(pooled, 1), s1[...]).astype(BF)


def deep_kernel(
    pos, own, up1, down1, up2, down2, skip0, skip1,
    t_in2, t_rec2, t_in3, t_rec3, t_in4, t_rec4,
    t_dec3, t_dec2, t_dec1, t_dec0, t_out,
    s2, s3, u3, u2, u1, u0,
    out, final,
    w, xa2, xa3, x3, xa4, xd1, xd0, d0,
):
    dev, g = pos[0], pos[1]
    has_up = (dev > 0).astype(F32)
    has_down = (dev < 255).astype(F32)
    zero_block = jnp.zeros((BLOCK, 256), BF)
    w[0] = zero_block
    w[21] = zero_block
    w[5:9] = up1[...]
    w[9:13] = own[...]
    w[13:17] = down1[...]
    at = 0
    for f in range(FRAMES):
        for d in range(4):
            if d >= f:
                w[1 + d, f * C1 : f * C1 + C1] = up2[at : at + C1]
                w[17 + 3 - d, f * C1 : f * C1 + C1] = down2[at : at + C1]
                at += C1
            else:
                w[1 + d, f * C1 : f * C1 + C1] = jnp.zeros((C1, 256), BF)
                w[17 + 3 - d, f * C1 : f * C1 + C1] = jnp.zeros((C1, 256), BF)
    for d in range(4):
        w[1 + d, XROWS : XROWS + C2] = up2[at : at + C2]
        w[17 + 3 - d, XROWS : XROWS + C2] = down2[at : at + C2]
        at += C2
    for d in range(4):
        if d >= 1:
            w[1 + d, XROWS + C2 :] = up2[at : at + 48]
            w[17 + 3 - d, XROWS + C2 :] = down2[at : at + 48]
            at += 48
        else:
            w[1 + d, XROWS + C2 :] = jnp.zeros((48, 256), BF)
            w[17 + 3 - d, XROWS + C2 :] = jnp.zeros((48, 256), BF)

    def init2(i, carry):
        xa2[0, i, C2:] = w[i + g, XROWS : XROWS + C2]
        xa2[1, i] = jnp.zeros((2 * C2, 256), BF)
        return carry

    lax.fori_loop(0, 19, init2, 0)
    for part in range(2):
        xa3[part, 0] = jnp.zeros((2 * C3, 256), BF)
        xa3[part, 5] = jnp.zeros((2 * C3, 256), BF)
    x3[0] = jnp.zeros((C2, 256), BF)
    x3[5] = jnp.zeros((C2, 256), BF)

    lane48 = lanes((48, 256))
    for b in range(4):
        low = jnp.zeros((48, 256), F32)
        high = jnp.zeros((48, 256), F32)
        for i in range(4):
            src = w[4 * b - 8 + i + 9 + g, XROWS + C2 :].astype(F32)
            here = (lane48 >= 64 * i) & (lane48 < 64 * i + 64)
            low = jnp.where(here, pltpu.roll(src, 64 * i, 1) if i else src, low)
            shift = (64 * i - 128) % 256
            high = jnp.where(here, pltpu.roll(src, shift, 1) if shift else src, high)
        xa3[0, b + 1, C3 : C3 + 48] = low.astype(BF)
        xa3[0, b + 1, C3 + 48 :] = high[:32].astype(BF)
    low = jnp.zeros((48, 256), F32)
    high = jnp.zeros((48, 256), F32)
    top = jnp.zeros((16, 256), F32)
    for k in range(-6, 7):
        src = w[k + 9 + g, XROWS + C2 :].astype(F32)
        first = 16 * (k + 8)
        here = (lane48 >= first) & (lane48 < first + 16)
        low = jnp.where(here, pltpu.roll(src, (first - 64) % 256, 1), low)
        high = jnp.where(here, pltpu.roll(src, (first - 192) % 256, 1), high)
        top = jnp.where(here[:16], pltpu.roll(src[:16], (first - 80) % 256, 1), top)
    xa4[C4 : C4 + 48] = low.astype(BF)
    xa4[C4 + 48 : C4 + 96] = high.astype(BF)
    xa4[C4 + 96 :] = top.astype(BF)

    lane1 = lanes((1, 256))

    def in_image(first, lane_device):
        d = dev + first + lane_device
        return ((d >= 0) & (d < 256)).astype(F32)

    mask3 = [in_image(4 * b - 8, lane1 // 64) for b in range(4)]
    mask4 = in_image(-8, lane1 // 16)
    mask3d = in_image(-2, lane1 // 64)

    for f in range(FRAMES):
        now, new = f % 2, (f + 1) % 2

        def in2(i, f=f, now=now):
            k = i - (8 - f)
            rows = slice(f * C1, f * C1 + C1)
            p = k + 9 + g
            rhs = three_rows(w[p - 1, rows], w[p, rows], w[p + 1, rows], 64)
            v = act(join_columns(dot(t_in2[...], rhs), C2, 64))
            keep = ((dev + k >= 0) & (dev + k < 256)).astype(F32)
            v = (v * keep).astype(BF)

            def store():
                xa2[now, k + 9, :C2] = v

            return store

        rounds(17 - 2 * f, in2, GROUP)

        def rec2(i, f=f, now=now, new=new):
            k = i - (7 - f)
            p = k + 9
            rhs = three_rows(xa2[now, p - 1], xa2[now, p], xa2[now, p + 1], 64)
            v = act(join_columns(dot(t_rec2[...], rhs), C2, 64))
            keep = ((dev + k >= 0) & (dev + k < 256)).astype(F32)
            v = (v * keep).astype(BF)

            def store():
                xa2[new, p, C2:] = v

            return store

        rounds(15 - 2 * f, rec2, GROUP)

        for b in range(4):
            pooled = [
                pair_max(xa2[new, 4 * b - 8 + i + 9, C2:].astype(F32), 64).astype(BF)
                for i in range(4)
            ]
            x3[b + 1] = dot(jnp.concatenate(pooled, 1), s2[...]).astype(BF)

        for b in range(1 if f == 3 else 0, 4):
            rhs = three_rows(x3[b], x3[b + 1], x3[b + 2], 32)
            v = act(join_columns(dot(t_in3[...], rhs), C3, 32))
            xa3[now, b + 1, :C3] = (v * mask3[b]).astype(BF)
        for b in range((0, 0, 1, 1)[f], (4, 4, 4, 3)[f]):
            rhs = three_rows(xa3[now, b], xa3[now, b + 1], xa3[now, b + 2], 32)
            v = act(join_columns(dot(t_rec3[...], rhs), C3, 32))
            xa3[new, b + 1, C3:] = (v * mask3[b]).astype(BF)

        pooled = [pair_max(xa3[new, b + 1, C3:].astype(F32), 32).astype(BF) for b in range(4)]
        x4 = dot(jnp.concatenate(pooled, 1), s3[...]).astype(BF)

        v = act(join_columns(dot(t_in4[...], three_rows_alone(x4, 16)), C4, 16))
        xa4[:C4] = (v * mask4).astype(BF)
        v = act(join_columns(dot(t_rec4[...], three_rows_alone(xa4[...], 16)), C4, 16))
        s4 = (v * mask4).astype(BF)
        xa4[C4:] = s4
        if f == FRAMES - 1:
            final[...] = s4

        skip3 = jnp.concatenate([xa3[new, 2, C3:][:, 128:], xa3[new, 3, C3:][:, :128]], 1)
        both = jnp.concatenate([dot(s4, u3[...]).astype(BF), skip3], 0)
        v = act(join_columns(dot(t_dec3[...], three_rows_alone(both, 32)), C3, 32))
        d3 = (v * mask3d).astype(BF)

        up = dot(d3, u2[...]).astype(BF)
        parts = [
            jnp.concatenate([up[:, 256 * j : 256 * j + 256], xa2[new, 8 + j, C2:]], 0)
            for j in range(3)
        ]
        d2 = []
        for j in range(3):
            rhs = three_rows(parts[max(j - 1, 0)], parts[j], parts[min(j + 1, 2)], 64)
            v = act(join_columns(dot(t_dec2[...], rhs), C2, 64))
            keep = (has_up, 1.0, has_down)[j]
            d2.append((v * keep).astype(BF))

        for j, low, first in ((0, 3, 0), (1, 0, 2), (2, 0, 10)):
            up = dot(d2[j], u1[...]).astype(BF)
            for r in range(low, 4 if j == 0 else (4 if j == 1 else 1)):
                row = first + 2 * (r - low)
                piece = up[:, 128 * r : 128 * r + 128]
                xd1[row, :C2] = piece
                xd1[row + 1, :C2] = piece
        xd1[:, C2:] = skip1[f]
        d1 = []
        for i in range(5):
            left = xd1[2 * i : 2 * i + 3].reshape(3 * (C1 + C2), 128)
            right = xd1[2 * i + 1 : 2 * i + 4].reshape(3 * (C1 + C2), 128)
            v = act(join_columns(dot(t_dec1[...], jnp.concatenate([left, right], 1)), C1, 128))
            first, second = v[:, :128], v[:, 128:]
            if i == 0:
                first = first * has_up
            if i == 4:
                second = second * has_down
            d1 += [first.astype(BF), second.astype(BF)]

        up = dot(jnp.concatenate(d1, 0), u0[...]).astype(BF)
        for j in range(10):
            piece = up[j * C1 : j * C1 + C1]
            xd0[2 * j, :C1] = piece
            xd0[2 * j + 1, :C1] = piece
        xd0[:, C1:] = skip0[f]

        def dec0(i):
            rhs = xd0[pl.ds(i, 3)].reshape(3 * (C0 + C1), 256)
            v = act(join_columns(dot(t_dec0[...], rhs), C0, 256))
            keep = jnp.where(i == 0, has_up, jnp.where(i == 17, has_down, 1.0))
            v = (v * keep).astype(BF)

            def store():
                d0[i] = v

            return store

        rounds(18, dec0, GROUP)

        for r in range(16):
            y = dot(t_out[...], d0[r : r + 3].reshape(3 * C0, 256))
            v = join_columns(y, 8, 256)
            for o in range(3):
                out[f, o, r : r + 1, :] = v[o : o + 1]


def shifted(value, axis, by):
    peers = lax.axis_size(axis)
    pairs = [(i, i + by) for i in range(peers) if 0 <= i + by < peers]
    return lax.ppermute(value, axis, pairs)


def per_device(
    noisy, state_0, state_1, state_2, state_3, state_4,
    enc_in_0, enc_in_1, enc_in_2, enc_in_3, enc_in_4,
    enc_rec_0, enc_rec_1, enc_rec_2, enc_rec_3, enc_rec_4,
    dec_0, dec_1, dec_2, dec_3, out_weight,
):
    grp = lax.axis_index("grp")
    dev = lax.axis_index("tile") * lax.axis_size("grp") + grp
    pos = jnp.stack([dev, grp]).astype(jnp.int32)

    own = jnp.concatenate(
        [
            jnp.pad(noisy.transpose(0, 2, 1, 3), ((0, 0), (0, 0), (0, 1), (0, 0))).reshape(512, 256),
            state_0.transpose(1, 0, 2).reshape(512, 256),
            jnp.pad(state_1.reshape(43, 4, 2, 128).transpose(1, 0, 2, 3), ((0, 0), (0, 5), (0, 0), (0, 0))).reshape(4 * C1, 256),
        ],
        0,
    )
    up = shifted(own, AXES, 1)
    down = shifted(own, AXES, -1)

    three = jnp.pad(state_3.reshape(76, 64), ((0, 20), (0, 0))).reshape(2, 48, 64)
    four = jnp.pad(state_4.reshape(101, 16), ((0, 43), (0, 0))).reshape(3, 48, 16)
    gap = jnp.zeros((48, 32), BF)
    rest = jnp.concatenate(
        [
            jnp.pad(state_2.reshape(57, 256), ((0, 7), (0, 0))),
            jnp.concatenate([three[0], four[0], four[2], gap, three[1], four[1], gap, gap[:, :16]], 1),
        ],
        0,
    )

    sel = selections()
    t_in0 = two_rows(taps(enc_in_0, C0, [(7, 8)]), 8)
    t_rec0 = two_rows(taps(enc_rec_0, C0, [(32, C0), (32, C0)]), 2 * C0)
    t_in1 = taps(enc_in_1, C1, [(32, C0)])
    t_rec1 = taps(enc_rec_1, C1, [(43, C1), (43, C1)])
    t_in2 = taps(enc_in_2, C2, [(43, C1)])
    t_rec2 = taps(enc_rec_2, C2, [(57, C2), (57, C2)])
    t_in3 = taps(enc_in_3, C3, [(57, C2)])
    t_rec3 = taps(enc_rec_3, C3, [(76, C3), (76, C3)])
    t_in4 = taps(enc_in_4, C4, [(76, C3)])
    t_rec4 = taps(enc_rec_4, C4, [(101, C4), (101, C4)])
    t_dec3 = taps(dec_3, C3, [(101, C4), (76, C3)])
    t_dec2 = taps(dec_2, C2, [(76, C3), (57, C2)])
    t_dec1 = taps(dec_1, C1, [(57, C2), (43, C1)])
    t_dec0 = taps(dec_0, C0, [(43, C1), (32, C0)])
    t_out = taps(out_weight, 8, [(32, C0)])

    smem = pl.BlockSpec(memory_space=pltpu.SMEM)
    vmem = pl.BlockSpec(memory_space=pltpu.VMEM)
    params = pltpu.CompilerParams(vmem_limit_bytes=VMEM)

    block, skip0, skip1 = pl.pallas_call(
        fine_kernel,
        out_shape=(
            jax.ShapeDtypeStruct((BLOCK, 256), BF),
            jax.ShapeDtypeStruct((FRAMES, 20, C0, 256), BF),
            jax.ShapeDtypeStruct((FRAMES, 12, C1, 128), BF),
        ),
        in_specs=[smem] + [vmem] * 10,
        out_specs=(vmem, vmem, vmem),
        scratch_shapes=[
            pltpu.VMEM((FRAMES, 24, 16, 256), BF),
            pltpu.VMEM((2, 48, 2 * C0, 256), BF),
            pltpu.VMEM((22, C0, 256), BF),
            pltpu.VMEM((22, C0, 128), BF),
            pltpu.VMEM((2, 24, 2 * C1, 128), BF),
        ],
        compiler_params=params,
        name="fine",
    )(pos, own, up, down, rest, t_in0, t_rec0, t_in1, t_rec1, sel["s0"], sel["s1"])

    tile = lax.all_gather(block, "grp", axis=0)
    up1 = shifted(tile, "tile", 1)
    down1 = shifted(tile, "tile", -1)

    def trimmed(order):
        pieces = [
            tile[d, f * C1 : f * C1 + C1] for f in range(FRAMES) for i, d in enumerate(order) if i >= f
        ]
        pieces += [tile[d, XROWS : XROWS + C2] for d in order]
        pieces += [tile[d, XROWS + C2 :] for d in order[1:]]
        return jnp.concatenate(pieces, 0)

    up2 = shifted(trimmed((0, 1, 2, 3)), "tile", 2)
    down2 = shifted(trimmed((3, 2, 1, 0)), "tile", -2)

    denoised, final = pl.pallas_call(
        deep_kernel,
        out_shape=(
            jax.ShapeDtypeStruct((FRAMES, 3, 16, 256), F32),
            jax.ShapeDtypeStruct((C4, 256), BF),
        ),
        in_specs=[smem] + [vmem] * 24,
        out_specs=(vmem, vmem),
        scratch_shapes=[
            pltpu.VMEM((22, BLOCK, 256), BF),
            pltpu.VMEM((2, 19, 2 * C2, 256), BF),
            pltpu.VMEM((2, 6, 2 * C3, 256), BF),
            pltpu.VMEM((6, C2, 256), BF),
            pltpu.VMEM((2 * C4, 256), BF),
            pltpu.VMEM((12, C1 + C2, 128), BF),
            pltpu.VMEM((20, C0 + C1, 256), BF),
            pltpu.VMEM((18, C0, 256), BF),
        ],
        compiler_params=params,
        name="deep",
    )(
        pos, tile, up1, down1, up2, down2, skip0, skip1,
        t_in2, t_rec2, t_in3, t_rec3, t_in4, t_rec4,
        t_dec3, t_dec2, t_dec1, t_dec0, t_out,
        sel["s2"], sel["s3"], sel["u3"], sel["u2"], sel["u1"], sel["u0"],
    )
    return denoised, final[:101, 128:144].reshape(101, 1, 16)


def solution(mesh):
    rows3 = P(None, None, AXES, None)
    rows2 = P(None, AXES, None)
    return jax.shard_map(
        per_device,
        mesh=mesh,
        in_specs=(rows3,) + (rows2,) * 5 + (P(),) * 15,
        out_specs=(rows3, rows2),
        check_vma=False,
    )
```

```python
import functools

import jax
import jax.numpy as jnp
import numpy as np
from jax import lax
from jax.experimental import pallas as pl
from jax.experimental.pallas import tpu as pltpu
from jax.sharding import PartitionSpec as P

BF = jnp.bfloat16
F32 = jnp.float32
AXES = ("tile", "grp")
FRAMES = 4
C0, C1, C2, C3, C4 = 32, 48, 64, 80, 112
X_AT = (C2, C2 + C1 + 48, C2 + 2 * C1 + 48, C2 + 3 * C1 + 48)
REST_AT = C2 + C1
BLOCK = C2 + 48 + FRAMES * C1
PREFIX = (X_AT[0] + C1, X_AT[1] + C1, X_AT[2] + C1, X_AT[3] + C1)
VMEM = 56 * 1024 * 1024
GROUP = 12
GROUP2 = 6


SHAPES = {
    "rec0": (C0, 2, ((32, C0), (32, C0))),
    "in1": (C1, 1, ((32, C0),)),
    "rec1": (C1, 1, ((43, C1), (43, C1))),
    "in2": (C2, 1, ((43, C1),)),
    "rec2": (C2, 1, ((57, C2), (57, C2))),
    "in3": (C3, 1, ((57, C2),)),
    "rec3": (C3, 1, ((76, C3), (76, C3))),
    "in4": (C4, 1, ((76, C3),)),
    "rec4": (C4, 1, ((101, C4), (101, C4))),
    "dec3": (C3, 1, ((101, C4), (76, C3))),
    "dec2": (C2, 1, ((76, C3), (57, C2))),
    "dec1": (C1, 1, ((57, C2), (43, C1))),
    "dec0": (C0, 1, ((43, C1), (32, C0))),
    "out": (8, 4, ((32, C0),)),
}


def taps_shape(name):
    if name == "in0":
        return (4 * C0, 144)
    pad, rows, parts = SHAPES[name]
    return (rows * 3 * pad, (rows + 2) * sum(p for _, p in parts))


def weights_kernel(*refs):
    count = len(SHAPES) + 1
    work = refs[-1]
    for name, raw, done in zip(("in0",) + tuple(SHAPES), refs[:count], refs[count:-1]):
        high, wide = taps_shape(name)
        work[:high, :wide] = jnp.zeros((high, wide), F32)
        o = raw.shape[1]
        for t in range(9):
            dr, dw = divmod(t, 3)
            k = raw[t].astype(F32)
            if name == "in0":
                for m in range(4):
                    p, odd = divmod(m + dr, 2)
                    at = p * 48 + dw * 16 + odd * 8
                    work[m * C0 : m * C0 + o, at : at + 7] = k
                continue
            pad, rows, parts = SHAPES[name]
            depth = sum(p for _, p in parts)
            for m in range(rows):
                row, at, first = (m * 3 + dw) * pad, (m + dr) * depth, 0
                for chans, wide_part in parts:
                    work[row : row + o, at : at + chans] = k[:, first : first + chans]
                    at += wide_part
                    first += chans
        done[...] = work[:high, :wide].astype(BF)


def pool_matrix(width, rows, lane_of):
    m = np.zeros((rows * width, 256), np.float32)
    for r in range(0, rows, 2):
        for c in range(0, width, 2):
            m[r * width + c, lane_of(r // 2, c // 2)] = 1
    return m


def selections():
    out = {}
    s0 = np.zeros((256, 128), np.float32)
    s0[2 * np.arange(128), np.arange(128)] = 1
    out["s0"] = s0
    s1 = np.zeros((4, 128, 256), np.float32)
    for j in range(4):
        s1[j, 2 * np.arange(64), 64 * j + np.arange(64)] = 1
    out["s1"] = s1.reshape(512, 256)
    out["s2"] = np.concatenate(
        [pool_matrix(64, 4, lambda r, c, i=i: 64 * i + 32 * r + c) for i in range(4)], 0
    )
    out["s3"] = np.concatenate(
        [pool_matrix(32, 8, lambda r, c, i=i: 64 * i + 16 * r + c) for i in range(4)], 0
    )
    u3 = np.zeros((256, 256), np.float32)
    for r in range(-4, 4):
        for c in range(32):
            u3[(r // 2 + 8) * 16 + c // 2, (r + 4) * 32 + c] = 1
    out["u3"] = u3
    u2 = np.zeros((256, 768), np.float32)
    for r in range(-4, 8):
        if -4 <= r // 2 < 4:
            for c in range(64):
                u2[(r // 2 + 4) * 32 + c // 2, (r + 4) * 64 + c] = 1
    out["u2"] = u2
    u1 = np.zeros((256, 512), np.float32)
    for r in range(4):
        for c in range(128):
            u1[r * 64 + c // 2, r * 128 + c] = 1
    out["u1"] = u1
    u0 = np.zeros((128, 256), np.float32)
    u0[np.arange(256) // 2, np.arange(256)] = 1
    out["u0"] = u0
    return {k: jnp.asarray(v, BF) for k, v in out.items()}


def dot(a, b):
    return jnp.dot(a, b, preferred_element_type=F32)


def lanes(shape):
    return lax.broadcasted_iota(jnp.int32, shape, 1)


def join_columns(y, out, width):
    count = y.shape[1]
    col = lanes((out, count)) & (width - 1)
    left = pltpu.roll(y[:out], 1, 1)
    right = pltpu.roll(y[2 * out :], count - 1, 1)
    return (
        y[out : 2 * out]
        + jnp.where(col == 0, 0.0, left)
        + jnp.where(col == width - 1, 0.0, right)
    )


def act(u):
    return jnp.maximum(u, 0.1 * u)


def three_rows(before, here, after, width):
    here32 = here.astype(F32)
    lane = lanes(here.shape)
    up = jnp.where(
        lane < width, pltpu.roll(before.astype(F32), width, 1), pltpu.roll(here32, width, 1)
    )
    down = jnp.where(
        lane >= 256 - width,
        pltpu.roll(after.astype(F32), 256 - width, 1),
        pltpu.roll(here32, 256 - width, 1),
    )
    return jnp.concatenate([up.astype(BF), here, down.astype(BF)], 0)


def three_rows_alone(here, width):
    here32 = here.astype(F32)
    up = pltpu.roll(here32, width, 1).astype(BF)
    down = pltpu.roll(here32, 256 - width, 1).astype(BF)
    return jnp.concatenate([up, here, down], 0)


def pair_max(value, width):
    count = value.shape[1]
    value = jnp.maximum(value, pltpu.roll(value, count - 1, 1))
    return jnp.maximum(value, pltpu.roll(value, count - width, 1))


def rounds(count, body, group):
    def run(first, size):
        for store in [body(first + j) for j in range(size)]:
            store()

    full = count // group

    def step(i, carry):
        run(i * group, group)
        return carry

    lax.fori_loop(0, full, step, 0)
    if count % group:
        run(full * group, count % group)


def fine_kernel(
    pos, own, up, down, rest, t_in0, t_rec0, t_in1, t_rec1, s0, s1,
    block, skip0, skip1, n, xs0, m0, x1, xs1,
):
    dev = pos[0]
    has_up = (dev > 0).astype(F32)
    has_down = (dev < 255).astype(F32)

    def place(src, part):
        lane = lanes((16, 256))
        for f in range(FRAMES):

            def columns(i, f=f):
                here = src[pl.ds(pl.multiple_of(f * 128 + 16 * i, 16), 16)]
                wide = here.astype(F32)
                left = jnp.where(lane == 0, 0.0, pltpu.roll(wide, 1, 1)).astype(BF)
                right = jnp.where(lane == 255, 0.0, pltpu.roll(wide, 255, 1)).astype(BF)

                def store():
                    n[f, part * 8 + i, :16] = left
                    n[f, part * 8 + i, 16:32] = here
                    n[f, part * 8 + i, 32:] = right

                return store

            rounds(8, columns, 8)
        xs0[0, part * 16 : part * 16 + 16, C0:] = src[512:1024].reshape(16, C0, 256)
        for j in range(4):
            two = src[1024 + j * C1 : 1024 + (j + 1) * C1]
            xs1[0, part * 8 + 2 * j, C1:] = two[:, :128]
            xs1[0, part * 8 + 2 * j + 1, C1:] = two[:, 128:]

    place(up, 0)
    place(own, 1)
    place(down, 2)

    for f in range(FRAMES):
        n[f, 24] = jnp.zeros((48, 256), BF)
    block[:C2] = rest[:C2]
    block[REST_AT : REST_AT + 48] = rest[C2:]

    for f in range(FRAMES):
        now, new = f % 2, (f + 1) % 2
        halo = 14 - 2 * f

        def in0(i, f=f, now=now, halo=halo):
            r = 16 - (halo + 1) + 4 * i
            p = (r - 1) // 2
            v = act(dot(t_in0[...], n[f, pl.ds(p, 3)].reshape(144, 256)))
            rows = []
            for m in range(4):
                row = r + m
                keep = jnp.where(row < 16, has_up, jnp.where(row >= 32, has_down, 1.0))
                rows.append((v[m * C0 : m * C0 + C0] * keep).astype(BF))

            def store():
                for m in range(4):
                    xs0[now, r + m, :C0] = rows[m]

            return store

        rounds((8 + halo + 2) // 2, in0, GROUP // 2)

        def rec0(i, f=f, now=now, new=new, halo=halo):
            r = 16 - halo + 2 * i
            rhs = xs0[now, pl.ds(r - 1, 4)].reshape(256, 256)
            y = dot(t_rec0[...], rhs)
            keep = jnp.where(r < 16, has_up, jnp.where(r >= 32, has_down, 1.0))
            both = []
            for m in range(2):
                v = act(join_columns(y[m * 96 : m * 96 + 96], C0, 256)) * keep
                both.append(v)
            top = jnp.maximum(both[0], both[1])
            top = jnp.maximum(top, pltpu.roll(top, 255, 1)).astype(BF)

            def store():
                for m in range(2):
                    xs0[new, r + m, C0:] = both[m].astype(BF)
                m0[i] = top

            return store

        rounds(8 + halo, rec0, GROUP)

        skip0[f] = xs0[new, 14:34, C0:]
        count = 8 + halo
        x1[:count] = dot(m0[:count].reshape(count * C0, 256), s0[...]).astype(BF).reshape(
            count, C0, 128
        )

        half = 5 - f

        def in1(i, f=f, now=now, half=half):
            left = x1[pl.ds(2 * i, 3)].reshape(3 * C0, 128)
            right = x1[pl.ds(2 * i + 1, 3)].reshape(3 * C0, 128)
            y = dot(t_in1[...], jnp.concatenate([left, right], 1))
            v = act(join_columns(y, C1, 128))
            both = []
            for m in range(2):
                row = 8 - (half + 1) + 2 * i + m
                keep = jnp.where(row < 8, has_up, jnp.where(row >= 16, has_down, 1.0))
                both.append((v[:, m * 128 : m * 128 + 128] * keep).astype(BF))

            def store():
                for m in range(2):
                    xs1[now, 8 - (half + 1) + 2 * i + m, :C1] = both[m]

            return store

        rounds(4 + half + 1, in1, GROUP)

        def rec1(i, f=f, now=now, new=new, half=half):
            r = 8 - half + 2 * i
            left = xs1[now, pl.ds(r - 1, 3)].reshape(6 * C1, 128)
            right = xs1[now, pl.ds(r, 3)].reshape(6 * C1, 128)
            y = dot(t_rec1[...], jnp.concatenate([left, right], 1))
            v = act(join_columns(y, C1, 128))
            both = []
            for m in range(2):
                row = r + m
                keep = jnp.where(row < 8, has_up, jnp.where(row >= 16, has_down, 1.0))
                both.append((v[:, m * 128 : m * 128 + 128] * keep).astype(BF))

            def store():
                for m in range(2):
                    xs1[new, r + m, C1:] = both[m]

            return store

        rounds(4 + half, rec1, GROUP)

        skip1[f] = xs1[new, 6:18, C1:]
        pooled = []
        for j in range(4):
            a = xs1[new, 8 + 2 * j, C1:].astype(F32)
            b = xs1[new, 9 + 2 * j, C1:].astype(F32)
            top = jnp.maximum(a, b)
            pooled.append(jnp.maximum(top, pltpu.roll(top, 127, 1)).astype(BF))
        block[X_AT[f] : X_AT[f] + C1] = dot(jnp.concatenate(pooled, 1), s1[...]).astype(BF)


def deep_kernel(
    pos, own, up1, down1, up2, down2, skip0, skip1,
    t_in2, t_rec2, t_in3, t_rec3, t_in4, t_rec4,
    t_dec3, t_dec2, t_dec1, t_dec0, t_out,
    s2, s3, u3, u2, u1, u0,
    out, final,
    w, xa2, xa3, x3, xa4, xd1, xd0, d0, keep4, keep3, keep2,
):
    dev, g = pos[0], pos[1]
    has_up = (dev > 0).astype(F32)
    has_down = (dev < 255).astype(F32)
    zero_block = jnp.zeros((BLOCK, 256), BF)
    w[0] = zero_block
    w[21] = zero_block
    w[5:9] = up1[...]
    w[9:13] = own[...]
    w[13:17] = down1[...]
    at = 0
    for d in range(4):
        size = PREFIX[d]
        for slot, src in ((1 + d, up2), (20 - d, down2)):
            w[slot, :size] = src[at : at + size]
            if size < BLOCK:
                w[slot, size:] = jnp.zeros((BLOCK - size, 256), BF)
        at += size

    def init2(i, carry):
        xa2[0, i, C2:] = w[i + g, :C2]
        xa2[1, i] = jnp.zeros((2 * C2, 256), BF)
        return carry

    lax.fori_loop(0, 19, init2, 0)
    for part in range(2):
        xa3[part, 0] = jnp.zeros((2 * C3, 256), BF)
        xa3[part, 5] = jnp.zeros((2 * C3, 256), BF)
    x3[0] = jnp.zeros((C2, 256), BF)
    x3[5] = jnp.zeros((C2, 256), BF)

    lane48 = lanes((48, 256))
    for b in range(4):
        low = jnp.zeros((48, 256), F32)
        high = jnp.zeros((48, 256), F32)
        for i in range(4):
            src = w[4 * b - 8 + i + 9 + g, REST_AT : REST_AT + 48].astype(F32)
            here = (lane48 >= 64 * i) & (lane48 < 64 * i + 64)
            low = jnp.where(here, pltpu.roll(src, 64 * i, 1) if i else src, low)
            shift = (64 * i - 128) % 256
            high = jnp.where(here, pltpu.roll(src, shift, 1) if shift else src, high)
        xa3[0, b + 1, C3 : C3 + 48] = low.astype(BF)
        xa3[0, b + 1, C3 + 48 :] = high[:32].astype(BF)
    low = jnp.zeros((48, 256), F32)
    high = jnp.zeros((48, 256), F32)
    top = jnp.zeros((16, 256), F32)
    for k in range(-6, 7):
        src = w[k + 9 + g, REST_AT : REST_AT + 48].astype(F32)
        first = 16 * (k + 8)
        here = (lane48 >= first) & (lane48 < first + 16)
        low = jnp.where(here, pltpu.roll(src, (first - 64) % 256, 1), low)
        high = jnp.where(here, pltpu.roll(src, (first - 192) % 256, 1), high)
        top = jnp.where(here[:16], pltpu.roll(src[:16], (first - 80) % 256, 1), top)
    xa4[C4 : C4 + 48] = low.astype(BF)
    xa4[C4 + 48 : C4 + 96] = high.astype(BF)
    xa4[C4 + 96 :] = top.astype(BF)

    lane1 = lanes((1, 256))

    def in_image(first, lane_device):
        d = dev + first + lane_device
        return ((d >= 0) & (d < 256)).astype(F32)

    mask3 = [in_image(4 * b - 8, lane1 // 64) for b in range(4)]
    mask4 = in_image(-8, lane1 // 16)
    mask3d = in_image(-2, lane1 // 64)

    for f in range(FRAMES):
        now, new = f % 2, (f + 1) % 2

        def in2(i, f=f, now=now):
            k = i - (8 - f)
            rows = slice(X_AT[f], X_AT[f] + C1)
            p = k + 9 + g
            rhs = three_rows(w[p - 1, rows], w[p, rows], w[p + 1, rows], 64)
            v = act(join_columns(dot(t_in2[...], rhs), C2, 64))
            keep = ((dev + k >= 0) & (dev + k < 256)).astype(F32)
            v = (v * keep).astype(BF)

            def store():
                xa2[now, k + 9, :C2] = v

            return store

        rounds(17 - 2 * f, in2, GROUP2)

        def rec2(i, f=f, now=now, new=new):
            k = i - (7 - f)
            p = k + 9
            rhs = three_rows(xa2[now, p - 1], xa2[now, p], xa2[now, p + 1], 64)
            v = act(join_columns(dot(t_rec2[...], rhs), C2, 64))
            keep = ((dev + k >= 0) & (dev + k < 256)).astype(F32)
            v = (v * keep).astype(BF)

            def store():
                xa2[new, p, C2:] = v

            return store

        rounds(15 - 2 * f, rec2, GROUP2)

        for b in range(4):
            pooled = [
                pair_max(xa2[new, 4 * b - 8 + i + 9, C2:].astype(F32), 64).astype(BF)
                for i in range(4)
            ]
            x3[b + 1] = dot(jnp.concatenate(pooled, 1), s2[...]).astype(BF)

        for b in range(1 if f == 3 else 0, 4):
            rhs = three_rows(x3[b], x3[b + 1], x3[b + 2], 32)
            v = act(join_columns(dot(t_in3[...], rhs), C3, 32))
            xa3[now, b + 1, :C3] = (v * mask3[b]).astype(BF)
        for b in range((0, 0, 1, 1)[f], (4, 4, 4, 3)[f]):
            rhs = three_rows(xa3[now, b], xa3[now, b + 1], xa3[now, b + 2], 32)
            v = act(join_columns(dot(t_rec3[...], rhs), C3, 32))
            xa3[new, b + 1, C3:] = (v * mask3[b]).astype(BF)

        pooled = [pair_max(xa3[new, b + 1, C3:].astype(F32), 32).astype(BF) for b in range(4)]
        x4 = dot(jnp.concatenate(pooled, 1), s3[...]).astype(BF)

        v = act(join_columns(dot(t_in4[...], three_rows_alone(x4, 16)), C4, 16))
        xa4[:C4] = (v * mask4).astype(BF)
        v = act(join_columns(dot(t_rec4[...], three_rows_alone(xa4[...], 16)), C4, 16))
        s4 = (v * mask4).astype(BF)
        xa4[C4:] = s4
        if f == FRAMES - 1:
            final[...] = s4

        keep4[f] = s4
        keep3[f] = jnp.concatenate([xa3[new, 2, C3:][:, 128:], xa3[new, 3, C3:][:, :128]], 1)
        for k in range(3):
            keep2[f, k] = xa2[new, 8 + k, C2:]

    every = range(FRAMES)
    d3 = []
    for f in every:
        both = jnp.concatenate([dot(keep4[f], u3[...]).astype(BF), keep3[f]], 0)
        v = act(join_columns(dot(t_dec3[...], three_rows_alone(both, 32)), C3, 32))
        d3.append((v * mask3d).astype(BF))

    d2 = []
    for f in every:
        up = dot(d3[f], u2[...]).astype(BF)
        parts = [
            jnp.concatenate([up[:, 256 * j : 256 * j + 256], keep2[f, j]], 0) for j in range(3)
        ]
        for j in range(3):
            rhs = three_rows(parts[max(j - 1, 0)], parts[j], parts[min(j + 1, 2)], 64)
            v = act(join_columns(dot(t_dec2[...], rhs), C2, 64))
            keep = (has_up, 1.0, has_down)[j]
            d2.append((v * keep).astype(BF))

    for f in every:
        up = dot(jnp.concatenate(d2[3 * f : 3 * f + 3], 0), u1[...]).astype(BF)
        for j, low, high, first in ((0, 3, 4, 0), (1, 0, 4, 2), (2, 0, 1, 10)):
            for r in range(low, high):
                row = first + 2 * (r - low)
                piece = up[j * C2 : j * C2 + C2, 128 * r : 128 * r + 128]
                xd1[f, row, :C2] = piece
                xd1[f, row + 1, :C2] = piece
        xd1[f, :, C2:] = skip1[f]

    d1 = [[] for f in every]
    for f in every:
        for i in range(5):
            left = xd1[f, 2 * i : 2 * i + 3].reshape(3 * (C1 + C2), 128)
            right = xd1[f, 2 * i + 1 : 2 * i + 4].reshape(3 * (C1 + C2), 128)
            v = act(join_columns(dot(t_dec1[...], jnp.concatenate([left, right], 1)), C1, 128))
            first, second = v[:, :128], v[:, 128:]
            if i == 0:
                first = first * has_up
            if i == 4:
                second = second * has_down
            d1[f] += [first.astype(BF), second.astype(BF)]

    for f in every:
        up = dot(jnp.concatenate(d1[f], 0), u0[...]).astype(BF)
        for j in range(10):
            piece = up[j * C1 : j * C1 + C1]
            xd0[f, 2 * j, :C1] = piece
            xd0[f, 2 * j + 1, :C1] = piece
        xd0[f, :, C1:] = skip0[f]

    for f in every:

        def dec0(i, f=f):
            rhs = xd0[f, pl.ds(i, 3)].reshape(3 * (C0 + C1), 256)
            v = act(join_columns(dot(t_dec0[...], rhs), C0, 256))
            keep = jnp.where(i == 0, has_up, jnp.where(i == 17, has_down, 1.0))
            v = (v * keep).astype(BF)

            def store():
                d0[f, i] = v

            return store

        rounds(18, dec0, 18)

    for f in every:
        done = []
        for r in range(0, 16, 4):
            y = dot(t_out[...], d0[f, r : r + 6].reshape(6 * C0, 256))
            done += [join_columns(y[24 * m : 24 * m + 24], 8, 256) for m in range(4)]
        for r in range(16):
            for o in range(3):
                out[f, o, r : r + 1, :] = done[r][o : o + 1]


def pack_kernel(tile, up, down):
    at = 0
    for i, size in enumerate(PREFIX):
        up[at : at + size] = tile[i, :size]
        down[at : at + size] = tile[3 - i, :size]
        at += size


def shifted(value, axis, by):
    peers = lax.axis_size(axis)
    pairs = [(i, i + by) for i in range(peers) if 0 <= i + by < peers]
    return lax.ppermute(value, axis, pairs)


def per_device(
    noisy, state_0, state_1, state_2, state_3, state_4,
    enc_in_0, enc_in_1, enc_in_2, enc_in_3, enc_in_4,
    enc_rec_0, enc_rec_1, enc_rec_2, enc_rec_3, enc_rec_4,
    dec_0, dec_1, dec_2, dec_3, out_weight,
):
    grp = lax.axis_index("grp")
    dev = lax.axis_index("tile") * lax.axis_size("grp") + grp
    pos = jnp.stack([dev, grp]).astype(jnp.int32)

    own = jnp.concatenate(
        [
            jnp.pad(noisy.transpose(0, 2, 1, 3), ((0, 0), (0, 0), (0, 1), (0, 0))).reshape(512, 256),
            state_0.transpose(1, 0, 2).reshape(512, 256),
            jnp.pad(state_1.reshape(43, 4, 2, 128).transpose(1, 0, 2, 3), ((0, 0), (0, 5), (0, 0), (0, 0))).reshape(4 * C1, 256),
        ],
        0,
    )
    up = shifted(own, AXES, 1)
    down = shifted(own, AXES, -1)

    three = jnp.pad(state_3.reshape(76, 64), ((0, 20), (0, 0))).reshape(2, 48, 64)
    four = jnp.pad(state_4.reshape(101, 16), ((0, 43), (0, 0))).reshape(3, 48, 16)
    gap = jnp.zeros((48, 32), BF)
    rest = jnp.concatenate(
        [
            jnp.pad(state_2.reshape(57, 256), ((0, 7), (0, 0))),
            jnp.concatenate([three[0], four[0], four[2], gap, three[1], four[1], gap, gap[:, :16]], 1),
        ],
        0,
    )

    sel = selections()
    smem = pl.BlockSpec(memory_space=pltpu.SMEM)
    vmem = pl.BlockSpec(memory_space=pltpu.VMEM)
    params = pltpu.CompilerParams(vmem_limit_bytes=VMEM)

    raw = (
        enc_in_0, enc_rec_0, enc_in_1, enc_rec_1, enc_in_2, enc_rec_2, enc_in_3, enc_rec_3,
        enc_in_4, enc_rec_4, dec_3, dec_2, dec_1, dec_0, out_weight,
    )
    names = ("in0",) + tuple(SHAPES)
    (
        t_in0, t_rec0, t_in1, t_rec1, t_in2, t_rec2, t_in3, t_rec3,
        t_in4, t_rec4, t_dec3, t_dec2, t_dec1, t_dec0, t_out,
    ) = pl.pallas_call(
        weights_kernel,
        out_shape=[jax.ShapeDtypeStruct(taps_shape(name), BF) for name in names],
        scratch_shapes=[pltpu.VMEM((384, 768), F32)],
        cost_estimate=pl.CostEstimate(flops=0, bytes_accessed=20_000_000, transcendentals=0),
        compiler_params=params,
        name="weights",
    )(*raw)

    block, skip0, skip1 = pl.pallas_call(
        fine_kernel,
        out_shape=(
            jax.ShapeDtypeStruct((BLOCK, 256), BF),
            jax.ShapeDtypeStruct((FRAMES, 20, C0, 256), BF),
            jax.ShapeDtypeStruct((FRAMES, 12, C1, 128), BF),
        ),
        in_specs=[smem] + [vmem] * 10,
        out_specs=(vmem, vmem, vmem),
        scratch_shapes=[
            pltpu.VMEM((FRAMES, 25, 48, 256), BF),
            pltpu.VMEM((2, 50, 2 * C0, 256), BF),
            pltpu.VMEM((22, C0, 256), BF),
            pltpu.VMEM((22, C0, 128), BF),
            pltpu.VMEM((2, 24, 2 * C1, 128), BF),
        ],
        compiler_params=params,
        name="fine",
    )(pos, own, up, down, rest, t_in0, t_rec0, t_in1, t_rec1, sel["s0"], sel["s1"])

    tile = lax.all_gather(block, "grp", axis=0)
    up1 = shifted(tile, "tile", 1)
    down1 = shifted(tile, "tile", -1)

    outer = jax.ShapeDtypeStruct((sum(PREFIX), 256), BF)
    send_up, send_down = pl.pallas_call(
        pack_kernel,
        out_shape=(outer, outer),
        compiler_params=params,
        name="pack",
    )(tile)
    up2 = shifted(send_up, "tile", 2)
    down2 = shifted(send_down, "tile", -2)

    denoised, final = pl.pallas_call(
        deep_kernel,
        out_shape=(
            jax.ShapeDtypeStruct((FRAMES, 3, 16, 256), F32),
            jax.ShapeDtypeStruct((C4, 256), BF),
        ),
        in_specs=[smem] + [vmem] * 24,
        out_specs=(vmem, vmem),
        scratch_shapes=[
            pltpu.VMEM((22, BLOCK, 256), BF),
            pltpu.VMEM((2, 19, 2 * C2, 256), BF),
            pltpu.VMEM((2, 6, 2 * C3, 256), BF),
            pltpu.VMEM((6, C2, 256), BF),
            pltpu.VMEM((2 * C4, 256), BF),
            pltpu.VMEM((FRAMES, 12, C1 + C2, 128), BF),
            pltpu.VMEM((FRAMES, 20, C0 + C1, 256), BF),
            pltpu.VMEM((FRAMES, 18, C0, 256), BF),
            pltpu.VMEM((FRAMES, C4, 256), BF),
            pltpu.VMEM((FRAMES, C3, 256), BF),
            pltpu.VMEM((FRAMES, 3, C2, 256), BF),
        ],
        compiler_params=params,
        name="deep",
    )(
        pos, tile, up1, down1, up2, down2, skip0, skip1,
        t_in2, t_rec2, t_in3, t_rec3, t_in4, t_rec4,
        t_dec3, t_dec2, t_dec1, t_dec0, t_out,
        sel["s2"], sel["s3"], sel["u3"], sel["u2"], sel["u1"], sel["u0"],
    )
    return denoised, final[:101, 128:144].reshape(101, 1, 16)


def solution(mesh):
    rows3 = P(None, None, AXES, None)
    rows2 = P(None, AXES, None)
    return jax.shard_map(
        per_device,
        mesh=mesh,
        in_specs=(rows3,) + (rows2,) * 5 + (P(),) * 15,
        out_specs=(rows3, rows2),
        check_vma=False,
    )
```

```python
import functools

import jax
import jax.numpy as jnp
import numpy as np
from jax import lax
from jax.experimental import pallas as pl
from jax.experimental.pallas import tpu as pltpu
from jax.sharding import PartitionSpec as P

BF = jnp.bfloat16
F32 = jnp.float32
AXES = ("tile", "grp")
FRAMES = 4
C0, C1, C2, C3, C4 = 32, 48, 64, 80, 112
X_AT = (C2, C2 + C1 + 48, C2 + 2 * C1 + 48, C2 + 3 * C1 + 48)
REST_AT = C2 + C1
BLOCK = C2 + 48 + FRAMES * C1
PREFIX = (X_AT[0] + C1, X_AT[1] + C1, X_AT[2] + C1, X_AT[3] + C1)
VMEM = 56 * 1024 * 1024
GROUP = 12
GROUP2 = 6


SHAPES = {
    "rec0": (C0, 2, ((32, C0), (32, C0))),
    "in1": (C1, 1, ((32, C0),)),
    "rec1": (C1, 1, ((43, C1), (43, C1))),
    "in2": (C2, 1, ((43, C1),)),
    "rec2": (C2, 1, ((57, C2), (57, C2))),
    "in3": (C3, 1, ((57, C2),)),
    "rec3": (C3, 1, ((76, C3), (76, C3))),
    "in4": (C4, 1, ((76, C3),)),
    "rec4": (C4, 1, ((101, C4), (101, C4))),
    "dec3": (C3, 1, ((101, C4), (76, C3))),
    "dec2": (C2, 1, ((76, C3), (57, C2))),
    "dec1": (C1, 1, ((57, C2), (43, C1))),
    "dec0": (C0, 1, ((43, C1), (32, C0))),
    "out": (8, 4, ((32, C0),)),
}


def taps_shape(name):
    if name == "in0":
        return (4 * C0, 144)
    pad, rows, parts = SHAPES[name]
    return (rows * 3 * pad, (rows + 2) * sum(p for _, p in parts))


def weights_kernel(*refs):
    count = len(SHAPES) + 1
    work = refs[-1]
    for name, raw, done in zip(("in0",) + tuple(SHAPES), refs[:count], refs[count:-1]):
        high, wide = taps_shape(name)
        work[:high, :wide] = jnp.zeros((high, wide), F32)
        o = raw.shape[1]
        for t in range(9):
            dr, dw = divmod(t, 3)
            k = raw[t].astype(F32)
            if name == "in0":
                for m in range(4):
                    p, odd = divmod(m + dr, 2)
                    at = p * 48 + dw * 16 + odd * 8
                    work[m * C0 : m * C0 + o, at : at + 7] = k
                continue
            pad, rows, parts = SHAPES[name]
            depth = sum(p for _, p in parts)
            for m in range(rows):
                row, at, first = (m * 3 + dw) * pad, (m + dr) * depth, 0
                for chans, wide_part in parts:
                    work[row : row + o, at : at + chans] = k[:, first : first + chans]
                    at += wide_part
                    first += chans
        done[...] = work[:high, :wide].astype(BF)


def pool_matrix(width, rows, lane_of):
    m = np.zeros((rows * width, 256), np.float32)
    for r in range(0, rows, 2):
        for c in range(0, width, 2):
            m[r * width + c, lane_of(r // 2, c // 2)] = 1
    return m


def selections():
    out = {}
    s0 = np.zeros((256, 128), np.float32)
    s0[2 * np.arange(128), np.arange(128)] = 1
    out["s0"] = s0
    s1 = np.zeros((4, 128, 256), np.float32)
    for j in range(4):
        s1[j, 2 * np.arange(64), 64 * j + np.arange(64)] = 1
    out["s1"] = s1.reshape(512, 256)
    out["s2"] = np.concatenate(
        [pool_matrix(64, 4, lambda r, c, i=i: 64 * i + 32 * r + c) for i in range(4)], 0
    )
    out["s3"] = np.concatenate(
        [pool_matrix(32, 8, lambda r, c, i=i: 64 * i + 16 * r + c) for i in range(4)], 0
    )
    u3 = np.zeros((256, 256), np.float32)
    for r in range(-4, 4):
        for c in range(32):
            u3[(r // 2 + 8) * 16 + c // 2, (r + 4) * 32 + c] = 1
    out["u3"] = u3
    u2 = np.zeros((256, 768), np.float32)
    for r in range(-4, 8):
        if -4 <= r // 2 < 4:
            for c in range(64):
                u2[(r // 2 + 4) * 32 + c // 2, (r + 4) * 64 + c] = 1
    out["u2"] = u2
    u1 = np.zeros((256, 512), np.float32)
    for r in range(4):
        for c in range(128):
            u1[r * 64 + c // 2, r * 128 + c] = 1
    out["u1"] = u1
    u0 = np.zeros((128, 256), np.float32)
    u0[np.arange(256) // 2, np.arange(256)] = 1
    out["u0"] = u0
    return {k: jnp.asarray(v, BF) for k, v in out.items()}


def dot(a, b):
    return jnp.dot(a, b, preferred_element_type=F32)


def lanes(shape):
    return lax.broadcasted_iota(jnp.int32, shape, 1)


def join_columns(y, out, width):
    count = y.shape[1]
    col = lanes((out, count)) & (width - 1)
    left = pltpu.roll(y[:out], 1, 1)
    right = pltpu.roll(y[2 * out :], count - 1, 1)
    return (
        y[out : 2 * out]
        + jnp.where(col == 0, 0.0, left)
        + jnp.where(col == width - 1, 0.0, right)
    )


def act(u):
    return jnp.maximum(u, 0.1 * u)


def three_rows(before, here, after, width):
    here32 = here.astype(F32)
    lane = lanes(here.shape)
    up = jnp.where(
        lane < width, pltpu.roll(before.astype(F32), width, 1), pltpu.roll(here32, width, 1)
    )
    down = jnp.where(
        lane >= 256 - width,
        pltpu.roll(after.astype(F32), 256 - width, 1),
        pltpu.roll(here32, 256 - width, 1),
    )
    return jnp.concatenate([up.astype(BF), here, down.astype(BF)], 0)


def three_rows_alone(here, width):
    here32 = here.astype(F32)
    up = pltpu.roll(here32, width, 1).astype(BF)
    down = pltpu.roll(here32, 256 - width, 1).astype(BF)
    return jnp.concatenate([up, here, down], 0)


def pair_max(value, width):
    count = value.shape[1]
    value = jnp.maximum(value, pltpu.roll(value, count - 1, 1))
    return jnp.maximum(value, pltpu.roll(value, count - width, 1))


def rounds(count, body, group):
    def run(first, size):
        for store in [body(first + j) for j in range(size)]:
            store()

    full = count // group

    def step(i, carry):
        run(i * group, group)
        return carry

    lax.fori_loop(0, full, step, 0)
    if count % group:
        run(full * group, count % group)


def fine_kernel(
    pos, own, up, down, rest, t_in0, t_rec0, t_in1, t_rec1, s0, s1,
    block, skip0, skip1, n, xs0, m0, x1, xs1,
):
    dev = pos[0]
    has_up = (dev > 0).astype(F32)
    has_down = (dev < 255).astype(F32)

    def place(src, part):
        lane = lanes((16, 256))
        for f in range(FRAMES):

            def columns(i, f=f):
                here = src[pl.ds(pl.multiple_of(f * 128 + 16 * i, 16), 16)]
                wide = here.astype(F32)
                left = jnp.where(lane == 0, 0.0, pltpu.roll(wide, 1, 1)).astype(BF)
                right = jnp.where(lane == 255, 0.0, pltpu.roll(wide, 255, 1)).astype(BF)

                def store():
                    n[f, part * 8 + i, :16] = left
                    n[f, part * 8 + i, 16:32] = here
                    n[f, part * 8 + i, 32:] = right

                return store

            rounds(8, columns, 8)
        xs0[0, part * 16 : part * 16 + 16, C0:] = src[512:1024].reshape(16, C0, 256)
        for j in range(4):
            two = src[1024 + j * C1 : 1024 + (j + 1) * C1]
            xs1[0, part * 8 + 2 * j, C1:] = two[:, :128]
            xs1[0, part * 8 + 2 * j + 1, C1:] = two[:, 128:]

    place(up, 0)
    place(own, 1)
    place(down, 2)

    for f in range(FRAMES):
        n[f, 24] = jnp.zeros((48, 256), BF)
    block[:C2] = rest[:C2]
    block[REST_AT : REST_AT + 48] = rest[C2:]

    for f in range(FRAMES):
        now, new = f % 2, (f + 1) % 2
        halo = 14 - 2 * f

        def in0(i, f=f, now=now, halo=halo):
            r = 16 - (halo + 1) + 4 * i
            p = (r - 1) // 2
            v = act(dot(t_in0[...], n[f, pl.ds(p, 3)].reshape(144, 256)))
            rows = []
            for m in range(4):
                row = r + m
                keep = jnp.where(row < 16, has_up, jnp.where(row >= 32, has_down, 1.0))
                rows.append((v[m * C0 : m * C0 + C0] * keep).astype(BF))

            def store():
                for m in range(4):
                    xs0[now, r + m, :C0] = rows[m]

            return store

        rounds((8 + halo + 2) // 2, in0, GROUP // 2)

        def rec0(i, f=f, now=now, new=new, halo=halo):
            r = 16 - halo + 2 * i
            rhs = xs0[now, pl.ds(r - 1, 4)].reshape(256, 256)
            y = dot(t_rec0[...], rhs)
            keep = jnp.where(r < 16, has_up, jnp.where(r >= 32, has_down, 1.0))
            both = []
            for m in range(2):
                v = act(join_columns(y[m * 96 : m * 96 + 96], C0, 256)) * keep
                both.append(v)
            top = jnp.maximum(both[0], both[1])
            top = jnp.maximum(top, pltpu.roll(top, 255, 1)).astype(BF)

            def store():
                for m in range(2):
                    xs0[new, r + m, C0:] = both[m].astype(BF)
                m0[i] = top

            return store

        rounds(8 + halo, rec0, GROUP)

        skip0[f] = xs0[new, 14:34, C0:]
        count = 8 + halo
        x1[:count] = dot(m0[:count].reshape(count * C0, 256), s0[...]).astype(BF).reshape(
            count, C0, 128
        )

        half = 5 - f

        def in1(i, f=f, now=now, half=half):
            left = x1[pl.ds(2 * i, 3)].reshape(3 * C0, 128)
            right = x1[pl.ds(2 * i + 1, 3)].reshape(3 * C0, 128)
            y = dot(t_in1[...], jnp.concatenate([left, right], 1))
            v = act(join_columns(y, C1, 128))
            both = []
            for m in range(2):
                row = 8 - (half + 1) + 2 * i + m
                keep = jnp.where(row < 8, has_up, jnp.where(row >= 16, has_down, 1.0))
                both.append((v[:, m * 128 : m * 128 + 128] * keep).astype(BF))

            def store():
                for m in range(2):
                    xs1[now, 8 - (half + 1) + 2 * i + m, :C1] = both[m]

            return store

        rounds(4 + half + 1, in1, GROUP)

        def rec1(i, f=f, now=now, new=new, half=half):
            r = 8 - half + 2 * i
            left = xs1[now, pl.ds(r - 1, 3)].reshape(6 * C1, 128)
            right = xs1[now, pl.ds(r, 3)].reshape(6 * C1, 128)
            y = dot(t_rec1[...], jnp.concatenate([left, right], 1))
            v = act(join_columns(y, C1, 128))
            both = []
            for m in range(2):
                row = r + m
                keep = jnp.where(row < 8, has_up, jnp.where(row >= 16, has_down, 1.0))
                both.append((v[:, m * 128 : m * 128 + 128] * keep).astype(BF))

            def store():
                for m in range(2):
                    xs1[new, r + m, C1:] = both[m]

            return store

        rounds(4 + half, rec1, GROUP)

        skip1[f] = xs1[new, 6:18, C1:]
        pooled = []
        for j in range(4):
            a = xs1[new, 8 + 2 * j, C1:].astype(F32)
            b = xs1[new, 9 + 2 * j, C1:].astype(F32)
            top = jnp.maximum(a, b)
            pooled.append(jnp.maximum(top, pltpu.roll(top, 127, 1)).astype(BF))
        block[X_AT[f] : X_AT[f] + C1] = dot(jnp.concatenate(pooled, 1), s1[...]).astype(BF)


def deep_kernel(
    pos, own, up1, down1, up2, down2, skip0, skip1,
    t_in2, t_rec2, t_in3, t_rec3, t_in4, t_rec4,
    t_dec3, t_dec2, t_dec1, t_dec0, t_out,
    s2, s3, u3, u2, u1, u0,
    out, final,
    w, xa2, xa3, x3, xa4, xd1, xd0, d0, keep2,
):
    dev, g = pos[0], pos[1]
    has_up = (dev > 0).astype(F32)
    has_down = (dev < 255).astype(F32)
    zero_block = jnp.zeros((BLOCK, 256), BF)
    w[0] = zero_block
    w[21] = zero_block
    w[5:9] = up1[...]
    w[9:13] = own[...]
    w[13:17] = down1[...]
    at = 0
    for d in range(4):
        size = PREFIX[d]
        for slot, src in ((1 + d, up2), (20 - d, down2)):
            w[slot, :size] = src[at : at + size]
            if size < BLOCK:
                w[slot, size:] = jnp.zeros((BLOCK - size, 256), BF)
        at += size

    def spread(buf, slot, first, value):
        size = value.shape[0]
        up = pltpu.roll(value, 64, 1).astype(BF)
        down = pltpu.roll(value, 192, 1).astype(BF)
        here = 2 * C2 + first
        below = 4 * C2 + first
        xa2[buf, slot, first : first + size, 64:] = up[:, 64:]
        xa2[buf, slot + 1, first : first + size, :64] = up[:, :64]
        xa2[buf, slot, here : here + size] = value.astype(BF)
        xa2[buf, slot, below : below + size, :192] = down[:, :192]
        xa2[buf, slot - 1, below : below + size, 192:] = down[:, 192:]

    def init2(i):
        value = w[i + g, :C2].astype(F32)

        def store():
            spread(0, i + 1, C2, value)
            xa2[1, i + 1, 3 * C2 : 4 * C2] = jnp.zeros((C2, 256), BF)

        return store

    rounds(19, init2, 10)
    for part in range(FRAMES + 1):
        for b in range(6):
            xa3[part, b] = jnp.zeros((2 * C3, 256), BF)
    for f in range(FRAMES):
        x3[f, 0] = jnp.zeros((C2, 256), BF)
        x3[f, 5] = jnp.zeros((C2, 256), BF)

    lane48 = lanes((48, 256))
    for b in range(4):
        low = jnp.zeros((48, 256), F32)
        high = jnp.zeros((48, 256), F32)
        for i in range(4):
            src = w[4 * b - 8 + i + 9 + g, REST_AT : REST_AT + 48].astype(F32)
            here = (lane48 >= 64 * i) & (lane48 < 64 * i + 64)
            low = jnp.where(here, pltpu.roll(src, 64 * i, 1) if i else src, low)
            shift = (64 * i - 128) % 256
            high = jnp.where(here, pltpu.roll(src, shift, 1) if shift else src, high)
        xa3[0, b + 1, C3 : C3 + 48] = low.astype(BF)
        xa3[0, b + 1, C3 + 48 :] = high[:32].astype(BF)
    low = jnp.zeros((48, 256), F32)
    high = jnp.zeros((48, 256), F32)
    top = jnp.zeros((16, 256), F32)
    for k in range(-6, 7):
        src = w[k + 9 + g, REST_AT : REST_AT + 48].astype(F32)
        first = 16 * (k + 8)
        here = (lane48 >= first) & (lane48 < first + 16)
        low = jnp.where(here, pltpu.roll(src, (first - 64) % 256, 1), low)
        high = jnp.where(here, pltpu.roll(src, (first - 192) % 256, 1), high)
        top = jnp.where(here[:16], pltpu.roll(src[:16], (first - 80) % 256, 1), top)
    xa4[0, C4 : C4 + 48] = low.astype(BF)
    xa4[0, C4 + 48 : C4 + 96] = high.astype(BF)
    xa4[0, C4 + 96 :] = top.astype(BF)

    lane1 = lanes((1, 256))

    def in_image(first, lane_device):
        d = dev + first + lane_device
        return ((d >= 0) & (d < 256)).astype(F32)

    mask3 = [in_image(4 * b - 8, lane1 // 64) for b in range(4)]
    mask4 = in_image(-8, lane1 // 16)
    mask3d = in_image(-2, lane1 // 64)

    for f in range(FRAMES):
        now, new = f % 2, (f + 1) % 2

        def in2(i, f=f, now=now):
            k = i - (8 - f)
            rows = slice(X_AT[f], X_AT[f] + C1)
            p = k + 9 + g
            rhs = three_rows(w[p - 1, rows], w[p, rows], w[p + 1, rows], 64)
            v = act(join_columns(dot(t_in2[...], rhs), C2, 64))
            keep = ((dev + k >= 0) & (dev + k < 256)).astype(F32)
            v = v * keep

            def store():
                spread(now, k + 10, 0, v)

            return store

        rounds(17 - 2 * f, in2, GROUP2)

        def rec2(i, f=f, now=now, new=new):
            k = i - (7 - f)
            p = k + 10
            v = act(join_columns(dot(t_rec2[...], xa2[now, p]), C2, 64))
            keep = ((dev + k >= 0) & (dev + k < 256)).astype(F32)
            v = v * keep

            def store():
                spread(new, p, C2, v)

            return store

        rounds(15 - 2 * f, rec2, GROUP2)

        for b in range(4):
            pooled = [
                pair_max(xa2[new, 4 * b + i + 2, 3 * C2 : 4 * C2].astype(F32), 64).astype(BF)
                for i in range(4)
            ]
            x3[f, b + 1] = dot(jnp.concatenate(pooled, 1), s2[...]).astype(BF)
        for k in range(3):
            keep2[f, k] = xa2[new, 9 + k, 3 * C2 : 4 * C2]

    every = range(FRAMES)
    for f in every:
        for b in range(1 if f == 3 else 0, 4):
            rhs = three_rows(x3[f, b], x3[f, b + 1], x3[f, b + 2], 32)
            v = act(join_columns(dot(t_in3[...], rhs), C3, 32))
            xa3[f, b + 1, :C3] = (v * mask3[b]).astype(BF)
    for f in every:
        for b in range((0, 0, 1, 1)[f], (4, 4, 4, 3)[f]):
            rhs = three_rows(xa3[f, b], xa3[f, b + 1], xa3[f, b + 2], 32)
            v = act(join_columns(dot(t_rec3[...], rhs), C3, 32))
            xa3[f + 1, b + 1, C3:] = (v * mask3[b]).astype(BF)

    x4 = []
    for f in every:
        pooled = [pair_max(xa3[f + 1, b + 1, C3:].astype(F32), 32).astype(BF) for b in range(4)]
        x4.append(dot(jnp.concatenate(pooled, 1), s3[...]).astype(BF))
    for f in every:
        v = act(join_columns(dot(t_in4[...], three_rows_alone(x4[f], 16)), C4, 16))
        xa4[f, :C4] = (v * mask4).astype(BF)
    for f in every:
        v = act(join_columns(dot(t_rec4[...], three_rows_alone(xa4[f], 16)), C4, 16))
        xa4[f + 1, C4:] = (v * mask4).astype(BF)
    final[...] = xa4[FRAMES, C4:]

    d3 = []
    for f in every:
        skip3 = jnp.concatenate([xa3[f + 1, 2, C3:][:, 128:], xa3[f + 1, 3, C3:][:, :128]], 1)
        both = jnp.concatenate([dot(xa4[f + 1, C4:], u3[...]).astype(BF), skip3], 0)
        v = act(join_columns(dot(t_dec3[...], three_rows_alone(both, 32)), C3, 32))
        d3.append((v * mask3d).astype(BF))

    d2 = []
    for f in every:
        up = dot(d3[f], u2[...]).astype(BF)
        parts = [
            jnp.concatenate([up[:, 256 * j : 256 * j + 256], keep2[f, j]], 0) for j in range(3)
        ]
        for j in range(3):
            rhs = three_rows(parts[max(j - 1, 0)], parts[j], parts[min(j + 1, 2)], 64)
            v = act(join_columns(dot(t_dec2[...], rhs), C2, 64))
            keep = (has_up, 1.0, has_down)[j]
            d2.append((v * keep).astype(BF))

    for f in every:
        up = dot(jnp.concatenate(d2[3 * f : 3 * f + 3], 0), u1[...]).astype(BF)
        for j, low, high, first in ((0, 3, 4, 0), (1, 0, 4, 2), (2, 0, 1, 10)):
            for r in range(low, high):
                row = first + 2 * (r - low)
                piece = up[j * C2 : j * C2 + C2, 128 * r : 128 * r + 128]
                xd1[f, row, :C2] = piece
                xd1[f, row + 1, :C2] = piece
        xd1[f, :, C2:] = skip1[f]

    d1 = [[] for f in every]
    for f in every:
        for i in range(5):
            left = xd1[f, 2 * i : 2 * i + 3].reshape(3 * (C1 + C2), 128)
            right = xd1[f, 2 * i + 1 : 2 * i + 4].reshape(3 * (C1 + C2), 128)
            v = act(join_columns(dot(t_dec1[...], jnp.concatenate([left, right], 1)), C1, 128))
            first, second = v[:, :128], v[:, 128:]
            if i == 0:
                first = first * has_up
            if i == 4:
                second = second * has_down
            d1[f] += [first.astype(BF), second.astype(BF)]

    for f in every:
        up = dot(jnp.concatenate(d1[f], 0), u0[...]).astype(BF)
        for j in range(10):
            piece = up[j * C1 : j * C1 + C1]
            xd0[f, 2 * j, :C1] = piece
            xd0[f, 2 * j + 1, :C1] = piece
        xd0[f, :, C1:] = skip0[f]

    for f in every:

        def dec0(i, f=f):
            rhs = xd0[f, pl.ds(i, 3)].reshape(3 * (C0 + C1), 256)
            v = act(join_columns(dot(t_dec0[...], rhs), C0, 256))
            keep = jnp.where(i == 0, has_up, jnp.where(i == 17, has_down, 1.0))
            v = (v * keep).astype(BF)

            def store():
                d0[f, i] = v

            return store

        rounds(18, dec0, 18)

    for f in every:
        done = []
        for r in range(0, 16, 4):
            y = dot(t_out[...], d0[f, r : r + 6].reshape(6 * C0, 256))
            done += [join_columns(y[24 * m : 24 * m + 24], 8, 256) for m in range(4)]
        for r in range(16):
            for o in range(3):
                out[f, o, r : r + 1, :] = done[r][o : o + 1]


def pack_kernel(tile, up, down):
    at = 0
    for i, size in enumerate(PREFIX):
        up[at : at + size] = tile[i, :size]
        down[at : at + size] = tile[3 - i, :size]
        at += size


def shifted(value, axis, by):
    peers = lax.axis_size(axis)
    pairs = [(i, i + by) for i in range(peers) if 0 <= i + by < peers]
    return lax.ppermute(value, axis, pairs)


def per_device(
    noisy, state_0, state_1, state_2, state_3, state_4,
    enc_in_0, enc_in_1, enc_in_2, enc_in_3, enc_in_4,
    enc_rec_0, enc_rec_1, enc_rec_2, enc_rec_3, enc_rec_4,
    dec_0, dec_1, dec_2, dec_3, out_weight,
):
    grp = lax.axis_index("grp")
    dev = lax.axis_index("tile") * lax.axis_size("grp") + grp
    pos = jnp.stack([dev, grp]).astype(jnp.int32)

    own = jnp.concatenate(
        [
            jnp.pad(noisy.transpose(0, 2, 1, 3), ((0, 0), (0, 0), (0, 1), (0, 0))).reshape(512, 256),
            state_0.transpose(1, 0, 2).reshape(512, 256),
            jnp.pad(state_1.reshape(43, 4, 2, 128).transpose(1, 0, 2, 3), ((0, 0), (0, 5), (0, 0), (0, 0))).reshape(4 * C1, 256),
        ],
        0,
    )
    up = shifted(own, AXES, 1)
    down = shifted(own, AXES, -1)

    three = jnp.pad(state_3.reshape(76, 64), ((0, 20), (0, 0))).reshape(2, 48, 64)
    four = jnp.pad(state_4.reshape(101, 16), ((0, 43), (0, 0))).reshape(3, 48, 16)
    gap = jnp.zeros((48, 32), BF)
    rest = jnp.concatenate(
        [
            jnp.pad(state_2.reshape(57, 256), ((0, 7), (0, 0))),
            jnp.concatenate([three[0], four[0], four[2], gap, three[1], four[1], gap, gap[:, :16]], 1),
        ],
        0,
    )

    sel = selections()
    smem = pl.BlockSpec(memory_space=pltpu.SMEM)
    vmem = pl.BlockSpec(memory_space=pltpu.VMEM)
    params = pltpu.CompilerParams(vmem_limit_bytes=VMEM)

    raw = (
        enc_in_0, enc_rec_0, enc_in_1, enc_rec_1, enc_in_2, enc_rec_2, enc_in_3, enc_rec_3,
        enc_in_4, enc_rec_4, dec_3, dec_2, dec_1, dec_0, out_weight,
    )
    names = ("in0",) + tuple(SHAPES)
    (
        t_in0, t_rec0, t_in1, t_rec1, t_in2, t_rec2, t_in3, t_rec3,
        t_in4, t_rec4, t_dec3, t_dec2, t_dec1, t_dec0, t_out,
    ) = pl.pallas_call(
        weights_kernel,
        out_shape=[jax.ShapeDtypeStruct(taps_shape(name), BF) for name in names],
        scratch_shapes=[pltpu.VMEM((384, 768), F32)],
        cost_estimate=pl.CostEstimate(flops=0, bytes_accessed=20_000_000, transcendentals=0),
        compiler_params=params,
        name="weights",
    )(*raw)

    block, skip0, skip1 = pl.pallas_call(
        fine_kernel,
        out_shape=(
            jax.ShapeDtypeStruct((BLOCK, 256), BF),
            jax.ShapeDtypeStruct((FRAMES, 20, C0, 256), BF),
            jax.ShapeDtypeStruct((FRAMES, 12, C1, 128), BF),
        ),
        in_specs=[smem] + [vmem] * 10,
        out_specs=(vmem, vmem, vmem),
        scratch_shapes=[
            pltpu.VMEM((FRAMES, 25, 48, 256), BF),
            pltpu.VMEM((2, 50, 2 * C0, 256), BF),
            pltpu.VMEM((22, C0, 256), BF),
            pltpu.VMEM((22, C0, 128), BF),
            pltpu.VMEM((2, 24, 2 * C1, 128), BF),
        ],
        compiler_params=params,
        name="fine",
    )(pos, own, up, down, rest, t_in0, t_rec0, t_in1, t_rec1, sel["s0"], sel["s1"])

    tile = lax.all_gather(block, "grp", axis=0)
    up1 = shifted(tile, "tile", 1)
    down1 = shifted(tile, "tile", -1)

    outer = jax.ShapeDtypeStruct((sum(PREFIX), 256), BF)
    send_up, send_down = pl.pallas_call(
        pack_kernel,
        out_shape=(outer, outer),
        compiler_params=params,
        name="pack",
    )(tile)
    up2 = shifted(send_up, "tile", 2)
    down2 = shifted(send_down, "tile", -2)

    denoised, final = pl.pallas_call(
        deep_kernel,
        out_shape=(
            jax.ShapeDtypeStruct((FRAMES, 3, 16, 256), F32),
            jax.ShapeDtypeStruct((C4, 256), BF),
        ),
        in_specs=[smem] + [vmem] * 24,
        out_specs=(vmem, vmem),
        scratch_shapes=[
            pltpu.VMEM((22, BLOCK, 256), BF),
            pltpu.VMEM((2, 21, 6 * C2, 256), BF),
            pltpu.VMEM((FRAMES + 1, 6, 2 * C3, 256), BF),
            pltpu.VMEM((FRAMES, 6, C2, 256), BF),
            pltpu.VMEM((FRAMES + 1, 2 * C4, 256), BF),
            pltpu.VMEM((FRAMES, 12, C1 + C2, 128), BF),
            pltpu.VMEM((FRAMES, 20, C0 + C1, 256), BF),
            pltpu.VMEM((FRAMES, 18, C0, 256), BF),
            pltpu.VMEM((FRAMES, 3, C2, 256), BF),
        ],
        compiler_params=params,
        name="deep",
    )(
        pos, tile, up1, down1, up2, down2, skip0, skip1,
        t_in2, t_rec2, t_in3, t_rec3, t_in4, t_rec4,
        t_dec3, t_dec2, t_dec1, t_dec0, t_out,
        sel["s2"], sel["s3"], sel["u3"], sel["u2"], sel["u1"], sel["u0"],
    )
    return denoised, final[:101, 128:144].reshape(101, 1, 16)


def solution(mesh):
    rows3 = P(None, None, AXES, None)
    rows2 = P(None, AXES, None)
    return jax.shard_map(
        per_device,
        mesh=mesh,
        in_specs=(rows3,) + (rows2,) * 5 + (P(),) * 15,
        out_specs=(rows3, rows2),
        check_vma=False,
    )
```

```python
import functools

import jax
import jax.numpy as jnp
import numpy as np
from jax import lax
from jax.experimental import pallas as pl
from jax.experimental.pallas import tpu as pltpu
from jax.sharding import PartitionSpec as P

BF = jnp.bfloat16
F32 = jnp.float32
AXES = ("tile", "grp")
FRAMES = 4
C0, C1, C2, C3, C4 = 32, 48, 64, 80, 112
X_AT = (C2, C2 + C1 + 48, C2 + 2 * C1 + 48, C2 + 3 * C1 + 48)
REST_AT = C2 + C1
BLOCK = C2 + 48 + FRAMES * C1
PREFIX = (X_AT[0] + C1, X_AT[1] + C1, X_AT[2] + C1, X_AT[3] + C1)
VMEM = 56 * 1024 * 1024
GROUP = 12
GROUP2 = 8


SHAPES = {
    "rec0": (C0, 2, ((32, C0), (32, C0))),
    "in1": (C1, 1, ((32, C0),)),
    "rec1": (C1, 1, ((43, C1), (43, C1))),
    "in2": (C2, 1, ((43, C1),)),
    "rec2": (C2, 1, ((57, C2), (57, C2))),
    "in3": (C3, 1, ((57, C2),)),
    "rec3": (C3, 1, ((76, C3), (76, C3))),
    "in4": (C4, 1, ((76, C3),)),
    "rec4": (C4, 1, ((101, C4), (101, C4))),
    "dec3": (C3, 1, ((101, C4), (76, C3))),
    "dec2": (C2, 1, ((76, C3), (57, C2))),
    "dec1": (C1, 1, ((57, C2), (43, C1))),
    "dec0": (C0, 1, ((43, C1), (32, C0))),
    "out": (8, 4, ((32, C0),)),
}


def taps_shape(name):
    if name == "in0":
        return (4 * C0, 144)
    pad, rows, parts = SHAPES[name]
    return (rows * 3 * pad, (rows + 2) * sum(p for _, p in parts))


def weights_kernel(*refs):
    count = len(SHAPES) + 1
    work = refs[-1]
    for name, raw, done in zip(("in0",) + tuple(SHAPES), refs[:count], refs[count:-1]):
        high, wide = taps_shape(name)
        work[:high, :wide] = jnp.zeros((high, wide), F32)
        o = raw.shape[1]
        for t in range(9):
            dr, dw = divmod(t, 3)
            k = raw[t].astype(F32)
            if name == "in0":
                for m in range(4):
                    p, odd = divmod(m + dr, 2)
                    at = p * 48 + dw * 16 + odd * 8
                    work[m * C0 : m * C0 + o, at : at + 7] = k
                continue
            pad, rows, parts = SHAPES[name]
            depth = sum(p for _, p in parts)
            for m in range(rows):
                row, at, first = (m * 3 + dw) * pad, (m + dr) * depth, 0
                for chans, wide_part in parts:
                    work[row : row + o, at : at + chans] = k[:, first : first + chans]
                    at += wide_part
                    first += chans
        done[...] = work[:high, :wide].astype(BF)


def pool_matrix(width, rows, lane_of):
    m = np.zeros((rows * width, 256), np.float32)
    for r in range(0, rows, 2):
        for c in range(0, width, 2):
            m[r * width + c, lane_of(r // 2, c // 2)] = 1
    return m


def selections():
    out = {}
    s0 = np.zeros((256, 128), np.float32)
    s0[2 * np.arange(128), np.arange(128)] = 1
    out["s0"] = s0
    s1 = np.zeros((4, 128, 256), np.float32)
    for j in range(4):
        s1[j, 2 * np.arange(64), 64 * j + np.arange(64)] = 1
    out["s1"] = s1.reshape(512, 256)
    out["s2"] = np.concatenate(
        [pool_matrix(64, 4, lambda r, c, i=i: 64 * i + 32 * r + c) for i in range(4)], 0
    )
    out["s3"] = np.concatenate(
        [pool_matrix(32, 8, lambda r, c, i=i: 64 * i + 16 * r + c) for i in range(4)], 0
    )
    u3 = np.zeros((256, 256), np.float32)
    for r in range(-4, 4):
        for c in range(32):
            u3[(r // 2 + 8) * 16 + c // 2, (r + 4) * 32 + c] = 1
    out["u3"] = u3
    u2 = np.zeros((256, 768), np.float32)
    for r in range(-4, 8):
        if -4 <= r // 2 < 4:
            for c in range(64):
                u2[(r // 2 + 4) * 32 + c // 2, (r + 4) * 64 + c] = 1
    out["u2"] = u2
    u1 = np.zeros((256, 512), np.float32)
    for r in range(4):
        for c in range(128):
            u1[r * 64 + c // 2, r * 128 + c] = 1
    out["u1"] = u1
    u0 = np.zeros((128, 256), np.float32)
    u0[np.arange(256) // 2, np.arange(256)] = 1
    out["u0"] = u0
    return {k: jnp.asarray(v, BF) for k, v in out.items()}


def dot(a, b):
    return jnp.dot(a, b, preferred_element_type=F32)


def lanes(shape):
    return lax.broadcasted_iota(jnp.int32, shape, 1)


def join_columns(y, out, width):
    count = y.shape[1]
    col = lanes((out, count)) & (width - 1)
    left = pltpu.roll(y[:out], 1, 1)
    right = pltpu.roll(y[2 * out :], count - 1, 1)
    return (
        y[out : 2 * out]
        + jnp.where(col == 0, 0.0, left)
        + jnp.where(col == width - 1, 0.0, right)
    )


def act(u):
    return jnp.maximum(u, 0.1 * u)


def three_rows(before, here, after, width):
    here32 = here.astype(F32)
    lane = lanes(here.shape)
    up = jnp.where(
        lane < width, pltpu.roll(before.astype(F32), width, 1), pltpu.roll(here32, width, 1)
    )
    down = jnp.where(
        lane >= 256 - width,
        pltpu.roll(after.astype(F32), 256 - width, 1),
        pltpu.roll(here32, 256 - width, 1),
    )
    return jnp.concatenate([up.astype(BF), here, down.astype(BF)], 0)


def three_rows_alone(here, width):
    here32 = here.astype(F32)
    up = pltpu.roll(here32, width, 1).astype(BF)
    down = pltpu.roll(here32, 256 - width, 1).astype(BF)
    return jnp.concatenate([up, here, down], 0)


def pair_max(value, width):
    count = value.shape[1]
    value = jnp.maximum(value, pltpu.roll(value, count - 1, 1))
    return jnp.maximum(value, pltpu.roll(value, count - width, 1))


def rounds(count, body, group):
    def run(first, size):
        for store in [body(first + j) for j in range(size)]:
            store()

    full = count // group

    def step(i, carry):
        run(i * group, group)
        return carry

    lax.fori_loop(0, full, step, 0)
    if count % group:
        run(full * group, count % group)


def fine_kernel(
    pos, own, up, down, rest, t_in0, t_rec0, t_in1, t_rec1, s0, s1,
    block, skip0, skip1, n, xs0, m0, x1, xs1,
):
    dev = pos[0]
    has_up = (dev > 0).astype(F32)
    has_down = (dev < 255).astype(F32)

    def place(src, part):
        lane = lanes((16, 256))
        for f in range(FRAMES):

            def columns(i, f=f):
                here = src[pl.ds(pl.multiple_of(f * 128 + 16 * i, 16), 16)]
                wide = here.astype(F32)
                left = jnp.where(lane == 0, 0.0, pltpu.roll(wide, 1, 1)).astype(BF)
                right = jnp.where(lane == 255, 0.0, pltpu.roll(wide, 255, 1)).astype(BF)

                def store():
                    n[f, part * 8 + i, :16] = left
                    n[f, part * 8 + i, 16:32] = here
                    n[f, part * 8 + i, 32:] = right

                return store

            rounds(8, columns, 8)
        xs0[0, part * 16 : part * 16 + 16, C0:] = src[512:1024].reshape(16, C0, 256)
        for j in range(4):
            two = src[1024 + j * C1 : 1024 + (j + 1) * C1]
            xs1[0, part * 8 + 2 * j, C1:] = two[:, :128]
            xs1[0, part * 8 + 2 * j + 1, C1:] = two[:, 128:]

    place(up, 0)
    place(own, 1)
    place(down, 2)

    for f in range(FRAMES):
        n[f, 24] = jnp.zeros((48, 256), BF)
    block[:C2] = rest[:C2]
    block[REST_AT : REST_AT + 48] = rest[C2:]

    for f in range(FRAMES):
        now, new = f % 2, (f + 1) % 2
        halo = 14 - 2 * f

        def in0(i, f=f, now=now, halo=halo):
            r = 16 - (halo + 1) + 4 * i
            p = (r - 1) // 2
            v = act(dot(t_in0[...], n[f, pl.ds(p, 3)].reshape(144, 256)))
            rows = []
            for m in range(4):
                row = r + m
                keep = jnp.where(row < 16, has_up, jnp.where(row >= 32, has_down, 1.0))
                rows.append((v[m * C0 : m * C0 + C0] * keep).astype(BF))

            def store():
                for m in range(4):
                    xs0[now, r + m, :C0] = rows[m]

            return store

        rounds((8 + halo + 2) // 2, in0, GROUP // 2)

        def rec0(i, f=f, now=now, new=new, halo=halo):
            r = 16 - halo + 2 * i
            rhs = xs0[now, pl.ds(r - 1, 4)].reshape(256, 256)
            y = dot(t_rec0[...], rhs)
            keep = jnp.where(r < 16, has_up, jnp.where(r >= 32, has_down, 1.0))
            both = []
            for m in range(2):
                v = act(join_columns(y[m * 96 : m * 96 + 96], C0, 256)) * keep
                both.append(v)
            top = jnp.maximum(both[0], both[1])
            top = jnp.maximum(top, pltpu.roll(top, 255, 1)).astype(BF)

            def store():
                for m in range(2):
                    xs0[new, r + m, C0:] = both[m].astype(BF)
                m0[i] = top

            return store

        rounds(8 + halo, rec0, GROUP)

        skip0[f] = xs0[new, 14:34, C0:]
        count = 8 + halo
        x1[:count] = dot(m0[:count].reshape(count * C0, 256), s0[...]).astype(BF).reshape(
            count, C0, 128
        )

        half = 5 - f

        def in1(i, f=f, now=now, half=half):
            left = x1[pl.ds(2 * i, 3)].reshape(3 * C0, 128)
            right = x1[pl.ds(2 * i + 1, 3)].reshape(3 * C0, 128)
            y = dot(t_in1[...], jnp.concatenate([left, right], 1))
            v = act(join_columns(y, C1, 128))
            both = []
            for m in range(2):
                row = 8 - (half + 1) + 2 * i + m
                keep = jnp.where(row < 8, has_up, jnp.where(row >= 16, has_down, 1.0))
                both.append((v[:, m * 128 : m * 128 + 128] * keep).astype(BF))

            def store():
                for m in range(2):
                    xs1[now, 8 - (half + 1) + 2 * i + m, :C1] = both[m]

            return store

        rounds(4 + half + 1, in1, GROUP)

        def rec1(i, f=f, now=now, new=new, half=half):
            r = 8 - half + 2 * i
            left = xs1[now, pl.ds(r - 1, 3)].reshape(6 * C1, 128)
            right = xs1[now, pl.ds(r, 3)].reshape(6 * C1, 128)
            y = dot(t_rec1[...], jnp.concatenate([left, right], 1))
            v = act(join_columns(y, C1, 128))
            both = []
            for m in range(2):
                row = r + m
                keep = jnp.where(row < 8, has_up, jnp.where(row >= 16, has_down, 1.0))
                both.append((v[:, m * 128 : m * 128 + 128] * keep).astype(BF))

            def store():
                for m in range(2):
                    xs1[new, r + m, C1:] = both[m]

            return store

        rounds(4 + half, rec1, GROUP)

        skip1[f] = xs1[new, 6:18, C1:]
        pooled = []
        for j in range(4):
            a = xs1[new, 8 + 2 * j, C1:].astype(F32)
            b = xs1[new, 9 + 2 * j, C1:].astype(F32)
            top = jnp.maximum(a, b)
            pooled.append(jnp.maximum(top, pltpu.roll(top, 127, 1)).astype(BF))
        block[X_AT[f] : X_AT[f] + C1] = dot(jnp.concatenate(pooled, 1), s1[...]).astype(BF)


def deep_kernel(
    pos, own, up1, down1, up2, down2, skip0, skip1,
    t_in2, t_rec2, t_in3, t_rec3, t_in4, t_rec4,
    t_dec3, t_dec2, t_dec1, t_dec0, t_out,
    s2, s3, u3, u2, u1, u0,
    out, final,
    w, xa2, xa3, x3, xa4, xd1, xd0, d0, keep2,
):
    dev, g = pos[0], pos[1]
    has_up = (dev > 0).astype(F32)
    has_down = (dev < 255).astype(F32)
    zero_block = jnp.zeros((BLOCK, 256), BF)
    w[0] = zero_block
    w[21] = zero_block
    w[5:9] = up1[...]
    w[9:13] = own[...]
    w[13:17] = down1[...]
    at = 0
    for d in range(4):
        size = PREFIX[d]
        for slot, src in ((1 + d, up2), (20 - d, down2)):
            w[slot, :size] = src[at : at + size]
            if size < BLOCK:
                w[slot, size:] = jnp.zeros((BLOCK - size, 256), BF)
        at += size

    def spread(buf, slot, first, value):
        size = value.shape[0]
        up = pltpu.roll(value, 64, 1).astype(BF)
        down = pltpu.roll(value, 192, 1).astype(BF)
        here = 2 * C2 + first
        below = 4 * C2 + first
        xa2[buf, slot, first : first + size, 64:] = up[:, 64:]
        xa2[buf, slot + 1, first : first + size, :64] = up[:, :64]
        xa2[buf, slot, here : here + size] = value.astype(BF)
        xa2[buf, slot, below : below + size, :192] = down[:, :192]
        xa2[buf, slot - 1, below : below + size, 192:] = down[:, 192:]

    def init2(i):
        value = w[i + g, :C2].astype(F32)

        def store():
            spread(0, i + 1, C2, value)
            xa2[1, i + 1, 3 * C2 : 4 * C2] = jnp.zeros((C2, 256), BF)

        return store

    rounds(19, init2, 10)
    for part in range(FRAMES + 1):
        for b in range(6):
            xa3[part, b] = jnp.zeros((2 * C3, 256), BF)
    for f in range(FRAMES):
        x3[f, 0] = jnp.zeros((C2, 256), BF)
        x3[f, 5] = jnp.zeros((C2, 256), BF)

    lane48 = lanes((48, 256))
    for b in range(4):
        low = jnp.zeros((48, 256), F32)
        high = jnp.zeros((48, 256), F32)
        for i in range(4):
            src = w[4 * b - 8 + i + 9 + g, REST_AT : REST_AT + 48].astype(F32)
            here = (lane48 >= 64 * i) & (lane48 < 64 * i + 64)
            low = jnp.where(here, pltpu.roll(src, 64 * i, 1) if i else src, low)
            shift = (64 * i - 128) % 256
            high = jnp.where(here, pltpu.roll(src, shift, 1) if shift else src, high)
        xa3[0, b + 1, C3 : C3 + 48] = low.astype(BF)
        xa3[0, b + 1, C3 + 48 :] = high[:32].astype(BF)
    low = jnp.zeros((48, 256), F32)
    high = jnp.zeros((48, 256), F32)
    top = jnp.zeros((16, 256), F32)
    for k in range(-6, 7):
        src = w[k + 9 + g, REST_AT : REST_AT + 48].astype(F32)
        first = 16 * (k + 8)
        here = (lane48 >= first) & (lane48 < first + 16)
        low = jnp.where(here, pltpu.roll(src, (first - 64) % 256, 1), low)
        high = jnp.where(here, pltpu.roll(src, (first - 192) % 256, 1), high)
        top = jnp.where(here[:16], pltpu.roll(src[:16], (first - 80) % 256, 1), top)
    xa4[0, C4 : C4 + 48] = low.astype(BF)
    xa4[0, C4 + 48 : C4 + 96] = high.astype(BF)
    xa4[0, C4 + 96 :] = top.astype(BF)

    lane1 = lanes((1, 256))

    def in_image(first, lane_device):
        d = dev + first + lane_device
        return ((d >= 0) & (d < 256)).astype(F32)

    mask3 = [in_image(4 * b - 8, lane1 // 64) for b in range(4)]
    mask4 = in_image(-8, lane1 // 16)
    mask3d = in_image(-2, lane1 // 64)

    for f in range(FRAMES):
        now, new = f % 2, (f + 1) % 2

        def in2(i, f=f, now=now):
            k = i - (8 - f)
            rows = slice(X_AT[f], X_AT[f] + C1)
            p = k + 9 + g
            rhs = three_rows(w[p - 1, rows], w[p, rows], w[p + 1, rows], 64)
            v = act(join_columns(dot(t_in2[...], rhs), C2, 64))
            keep = ((dev + k >= 0) & (dev + k < 256)).astype(F32)
            v = v * keep

            def store():
                spread(now, k + 10, 0, v)

            return store

        rounds(17 - 2 * f, in2, GROUP2)

        def rec2(i, f=f, now=now, new=new):
            k = i - (7 - f)
            p = k + 10
            v = act(join_columns(dot(t_rec2[...], xa2[now, p]), C2, 64))
            keep = ((dev + k >= 0) & (dev + k < 256)).astype(F32)
            v = v * keep

            def store():
                spread(new, p, C2, v)

            return store

        rounds(15 - 2 * f, rec2, GROUP2)

        for b in range(4):
            pooled = [
                pair_max(xa2[new, 4 * b + i + 2, 3 * C2 : 4 * C2].astype(F32), 64).astype(BF)
                for i in range(4)
            ]
            x3[f, b + 1] = dot(jnp.concatenate(pooled, 1), s2[...]).astype(BF)
        for k in range(3):
            keep2[f, k] = xa2[new, 9 + k, 3 * C2 : 4 * C2]

    every = range(FRAMES)
    for f in every:
        for b in range(1 if f == 3 else 0, 4):
            rhs = three_rows(x3[f, b], x3[f, b + 1], x3[f, b + 2], 32)
            v = act(join_columns(dot(t_in3[...], rhs), C3, 32))
            xa3[f, b + 1, :C3] = (v * mask3[b]).astype(BF)
    for f in every:
        for b in range((0, 0, 1, 1)[f], (4, 4, 4, 3)[f]):
            rhs = three_rows(xa3[f, b], xa3[f, b + 1], xa3[f, b + 2], 32)
            v = act(join_columns(dot(t_rec3[...], rhs), C3, 32))
            xa3[f + 1, b + 1, C3:] = (v * mask3[b]).astype(BF)

    x4 = []
    for f in every:
        pooled = [pair_max(xa3[f + 1, b + 1, C3:].astype(F32), 32).astype(BF) for b in range(4)]
        x4.append(dot(jnp.concatenate(pooled, 1), s3[...]).astype(BF))
    for f in every:
        v = act(join_columns(dot(t_in4[...], three_rows_alone(x4[f], 16)), C4, 16))
        xa4[f, :C4] = (v * mask4).astype(BF)
    for f in every:
        v = act(join_columns(dot(t_rec4[...], three_rows_alone(xa4[f], 16)), C4, 16))
        xa4[f + 1, C4:] = (v * mask4).astype(BF)
    final[...] = xa4[FRAMES, C4:]

    d3 = []
    for f in every:
        skip3 = jnp.concatenate([xa3[f + 1, 2, C3:][:, 128:], xa3[f + 1, 3, C3:][:, :128]], 1)
        both = jnp.concatenate([dot(xa4[f + 1, C4:], u3[...]).astype(BF), skip3], 0)
        v = act(join_columns(dot(t_dec3[...], three_rows_alone(both, 32)), C3, 32))
        d3.append((v * mask3d).astype(BF))

    d2 = []
    for f in every:
        up = dot(d3[f], u2[...]).astype(BF)
        parts = [
            jnp.concatenate([up[:, 256 * j : 256 * j + 256], keep2[f, j]], 0) for j in range(3)
        ]
        for j in range(3):
            rhs = three_rows(parts[max(j - 1, 0)], parts[j], parts[min(j + 1, 2)], 64)
            v = act(join_columns(dot(t_dec2[...], rhs), C2, 64))
            keep = (has_up, 1.0, has_down)[j]
            d2.append((v * keep).astype(BF))

    for f in every:
        up = dot(jnp.concatenate(d2[3 * f : 3 * f + 3], 0), u1[...]).astype(BF)
        for j, low, high, first in ((0, 3, 4, 0), (1, 0, 4, 2), (2, 0, 1, 10)):
            for r in range(low, high):
                row = first + 2 * (r - low)
                piece = up[j * C2 : j * C2 + C2, 128 * r : 128 * r + 128]
                xd1[f, row, :C2] = piece
                xd1[f, row + 1, :C2] = piece
        xd1[f, :, C2:] = skip1[f]

    d1 = [[] for f in every]
    for f in every:
        for i in range(5):
            left = xd1[f, 2 * i : 2 * i + 3].reshape(3 * (C1 + C2), 128)
            right = xd1[f, 2 * i + 1 : 2 * i + 4].reshape(3 * (C1 + C2), 128)
            v = act(join_columns(dot(t_dec1[...], jnp.concatenate([left, right], 1)), C1, 128))
            first, second = v[:, :128], v[:, 128:]
            if i == 0:
                first = first * has_up
            if i == 4:
                second = second * has_down
            d1[f] += [first.astype(BF), second.astype(BF)]

    for f in every:
        up = dot(jnp.concatenate(d1[f], 0), u0[...]).astype(BF)
        for j in range(10):
            piece = up[j * C1 : j * C1 + C1]
            xd0[f, 2 * j, :C1] = piece
            xd0[f, 2 * j + 1, :C1] = piece
        xd0[f, :, C1:] = skip0[f]

    for f in every:

        def dec0(i, f=f):
            rhs = xd0[f, pl.ds(i, 3)].reshape(3 * (C0 + C1), 256)
            v = act(join_columns(dot(t_dec0[...], rhs), C0, 256))
            keep = jnp.where(i == 0, has_up, jnp.where(i == 17, has_down, 1.0))
            v = (v * keep).astype(BF)

            def store():
                d0[f, i] = v

            return store

        rounds(18, dec0, 18)

    for f in every:
        done = []
        for r in range(0, 16, 4):
            y = dot(t_out[...], d0[f, r : r + 6].reshape(6 * C0, 256))
            done += [join_columns(y[24 * m : 24 * m + 24], 8, 256) for m in range(4)]
        for r in range(16):
            for o in range(3):
                out[f, o, r : r + 1, :] = done[r][o : o + 1]


def pack_kernel(tile, up, down):
    at = 0
    for i, size in enumerate(PREFIX):
        up[at : at + size] = tile[i, :size]
        down[at : at + size] = tile[3 - i, :size]
        at += size


def shifted(value, axis, by):
    peers = lax.axis_size(axis)
    pairs = [(i, i + by) for i in range(peers) if 0 <= i + by < peers]
    return lax.ppermute(value, axis, pairs)


def per_device(
    noisy, state_0, state_1, state_2, state_3, state_4,
    enc_in_0, enc_in_1, enc_in_2, enc_in_3, enc_in_4,
    enc_rec_0, enc_rec_1, enc_rec_2, enc_rec_3, enc_rec_4,
    dec_0, dec_1, dec_2, dec_3, out_weight,
):
    grp = lax.axis_index("grp")
    dev = lax.axis_index("tile") * lax.axis_size("grp") + grp
    pos = jnp.stack([dev, grp]).astype(jnp.int32)

    own = jnp.concatenate(
        [
            jnp.pad(noisy.transpose(0, 2, 1, 3), ((0, 0), (0, 0), (0, 1), (0, 0))).reshape(512, 256),
            state_0.transpose(1, 0, 2).reshape(512, 256),
            jnp.pad(state_1.reshape(43, 4, 2, 128).transpose(1, 0, 2, 3), ((0, 0), (0, 5), (0, 0), (0, 0))).reshape(4 * C1, 256),
        ],
        0,
    )
    up = shifted(own, AXES, 1)
    down = shifted(own, AXES, -1)

    three = jnp.pad(state_3.reshape(76, 64), ((0, 20), (0, 0))).reshape(2, 48, 64)
    four = jnp.pad(state_4.reshape(101, 16), ((0, 43), (0, 0))).reshape(3, 48, 16)
    gap = jnp.zeros((48, 32), BF)
    rest = jnp.concatenate(
        [
            jnp.pad(state_2.reshape(57, 256), ((0, 7), (0, 0))),
            jnp.concatenate([three[0], four[0], four[2], gap, three[1], four[1], gap, gap[:, :16]], 1),
        ],
        0,
    )

    sel = selections()
    smem = pl.BlockSpec(memory_space=pltpu.SMEM)
    vmem = pl.BlockSpec(memory_space=pltpu.VMEM)
    params = pltpu.CompilerParams(vmem_limit_bytes=VMEM)

    raw = (
        enc_in_0, enc_rec_0, enc_in_1, enc_rec_1, enc_in_2, enc_rec_2, enc_in_3, enc_rec_3,
        enc_in_4, enc_rec_4, dec_3, dec_2, dec_1, dec_0, out_weight,
    )
    names = ("in0",) + tuple(SHAPES)
    (
        t_in0, t_rec0, t_in1, t_rec1, t_in2, t_rec2, t_in3, t_rec3,
        t_in4, t_rec4, t_dec3, t_dec2, t_dec1, t_dec0, t_out,
    ) = pl.pallas_call(
        weights_kernel,
        out_shape=[jax.ShapeDtypeStruct(taps_shape(name), BF) for name in names],
        scratch_shapes=[pltpu.VMEM((384, 768), F32)],
        cost_estimate=pl.CostEstimate(flops=0, bytes_accessed=20_000_000, transcendentals=0),
        compiler_params=params,
        name="weights",
    )(*raw)

    block, skip0, skip1 = pl.pallas_call(
        fine_kernel,
        out_shape=(
            jax.ShapeDtypeStruct((BLOCK, 256), BF),
            jax.ShapeDtypeStruct((FRAMES, 20, C0, 256), BF),
            jax.ShapeDtypeStruct((FRAMES, 12, C1, 128), BF),
        ),
        in_specs=[smem] + [vmem] * 10,
        out_specs=(vmem, vmem, vmem),
        scratch_shapes=[
            pltpu.VMEM((FRAMES, 25, 48, 256), BF),
            pltpu.VMEM((2, 50, 2 * C0, 256), BF),
            pltpu.VMEM((22, C0, 256), BF),
            pltpu.VMEM((22, C0, 128), BF),
            pltpu.VMEM((2, 24, 2 * C1, 128), BF),
        ],
        compiler_params=params,
        name="fine",
    )(pos, own, up, down, rest, t_in0, t_rec0, t_in1, t_rec1, sel["s0"], sel["s1"])

    tile = lax.all_gather(block, "grp", axis=0)
    up1 = shifted(tile, "tile", 1)
    down1 = shifted(tile, "tile", -1)

    outer = jax.ShapeDtypeStruct((sum(PREFIX), 256), BF)
    send_up, send_down = pl.pallas_call(
        pack_kernel,
        out_shape=(outer, outer),
        compiler_params=params,
        name="pack",
    )(tile)
    up2 = shifted(send_up, "tile", 2)
    down2 = shifted(send_down, "tile", -2)

    denoised, final = pl.pallas_call(
        deep_kernel,
        out_shape=(
            jax.ShapeDtypeStruct((FRAMES, 3, 16, 256), F32),
            jax.ShapeDtypeStruct((C4, 256), BF),
        ),
        in_specs=[smem] + [vmem] * 24,
        out_specs=(vmem, vmem),
        scratch_shapes=[
            pltpu.VMEM((22, BLOCK, 256), BF),
            pltpu.VMEM((2, 21, 6 * C2, 256), BF),
            pltpu.VMEM((FRAMES + 1, 6, 2 * C3, 256), BF),
            pltpu.VMEM((FRAMES, 6, C2, 256), BF),
            pltpu.VMEM((FRAMES + 1, 2 * C4, 256), BF),
            pltpu.VMEM((FRAMES, 12, C1 + C2, 128), BF),
            pltpu.VMEM((FRAMES, 20, C0 + C1, 256), BF),
            pltpu.VMEM((FRAMES, 18, C0, 256), BF),
            pltpu.VMEM((FRAMES, 3, C2, 256), BF),
        ],
        compiler_params=params,
        name="deep",
    )(
        pos, tile, up1, down1, up2, down2, skip0, skip1,
        t_in2, t_rec2, t_in3, t_rec3, t_in4, t_rec4,
        t_dec3, t_dec2, t_dec1, t_dec0, t_out,
        sel["s2"], sel["s3"], sel["u3"], sel["u2"], sel["u1"], sel["u0"],
    )
    return denoised, final[:101, 128:144].reshape(101, 1, 16)


def solution(mesh):
    rows3 = P(None, None, AXES, None)
    rows2 = P(None, AXES, None)
    return jax.shard_map(
        per_device,
        mesh=mesh,
        in_specs=(rows3,) + (rows2,) * 5 + (P(),) * 15,
        out_specs=(rows3, rows2),
        check_vma=False,
    )
```
